256 devices in a mesh: sta: 128 (over y_lo, x, z, core), win: 2 (over y_hi).
Axes of the slice: x: 4, y: 4 (y_hi: 2, y_lo: 2; y = y_hi * 2 + y_lo), z: 8, core: 2. Of those that a mesh axis runs over, the one named last changes fastest.
Arguments:
- raw_traces: bfloat16 [2, 32768, 4096], P('win', 'sta'), may hold values from -6 to 6
- fir_taps: bfloat16 [127], replicated, may hold values from -0.5 to 0.5
- source_slot: int32 [16, 2048], P('win', 'sta'), may hold values from 0 to 255, as said below
- present: int32 [16, 2048], P('win', 'sta'), may hold values 0 or 1
- lag_start: int32 [2048, 2048], P('sta'), may hold values from -2048 to 1920
Outputs:
- correlations: float32 [2048, 2048, 128], P('sta', 'win')
The draws below stay inside these ranges and needn't reach their ends.
Inputs may be any that keep to these rules, and one draw needn't show every extreme that they name: `source_slot`: for each win index and each block of 16 stations on one sta index, the 128 entries are distinct; entry e names row e % 2 of the 2 rows that the file device with sta index e // 2 holds for this block. For every block, some file device holds 2 of its traces.
All inputs are finite; a program needn't handle non-finite values. No bound on the sum of `present` on one device may be relied on, other than what follows from the above.
Results may differ from the reference program's by a relative error of at most 0.0093.
Values may be sent and summed in bfloat16 or wider, within the bound.
No kernel may reach another device: no remote copies, remote signals or barrier semaphores. Data moves between devices by JAX's collectives and lax.ppermute only.
A program may use at most 128 MiB of HBM per device.

```python
import math
import jax
import jax.numpy as jnp
from jax import lax

L = 4096
TAPS = 127
FB = 64
BIN0 = 16
LAGW = 128
STD = 16
WDEV = 8
S = 2048
WINDOWS = 16
SLOTS = 256
CAP = 2
FILE_ROWS = 32768
N_STA = 128
N_WIN = 2


def draw_source_slot(key, part):
    traces_block = STD * WDEV

    def one_block(block_key):
        key_bias, key_full, key_rank, key_order = jax.random.split(block_key, 4)
        file_bias = jax.random.randint(key_bias, (N_STA,), 0, 3)
        fullest = jax.random.randint(key_full, (), 0, N_STA)
        file_bias = jnp.where(jnp.arange(N_STA) == fullest, 3, file_bias)
        slot_ids = jnp.arange(SLOTS, dtype=jnp.int32)
        rank_noise = jax.random.randint(key_rank, (SLOTS,), 0, 4096)
        scores = (file_bias[slot_ids // CAP] * 4096 + rank_noise) * SLOTS + slot_ids
        chosen = jnp.argsort(-scores)[:traces_block]
        return jax.random.permutation(key_order, chosen)
    block_keys = jax.random.split(jax.random.fold_in(key, 7), N_WIN * N_STA)
    slot_table = jax.vmap(one_block)(block_keys)
    slot_table = slot_table.reshape(N_WIN, N_STA, WDEV, STD).transpose(0, 2, 1, 3)
    return slot_table.reshape(WINDOWS, S).astype(jnp.int32)


def with_ends(entries, own_key, low, top_value):
    dims = entries.shape
    index_at = [jax.random.randint(jax.random.fold_in(own_key, axis), (), 0, dims[axis]) for axis in range(len(dims))]
    entries = entries.at[tuple(index_at)].set(low)
    longest = dims.index(max(dims))
    index_at[longest] = (index_at[longest] + 1) % dims[longest]
    return entries.at[tuple(index_at)].set(top_value)


def levels(rng, shape, shards, low, top_value):
    def one(axis_at, blocks):
        heights = jax.random.uniform(jax.random.fold_in(jax.random.fold_in(rng, 6), axis_at), (blocks,), jnp.float32, low / len(shards), top_value / len(shards))
        return jnp.repeat(jnp.exp(heights), shape[axis_at] // blocks).reshape((-1,) + (1,) * (len(shape) - axis_at - 1))

    factor_of = one(*shards[0])
    for cut in shards[1:]:
        factor_of = factor_of * one(*cut)
    return factor_of


def gaussian(own_key, dims, scale, limit, pieces=(), kind=jnp.bfloat16):
    array = jax.random.normal(own_key, dims, jnp.float32) * scale
    if len(pieces) > 0:
        array = levels(own_key, dims, pieces, -0.22, 0.18) * array
    return jnp.clip(array, min=-limit, max=limit).astype(kind)


def setup_inputs(seed: int = 0) -> dict:
    seeds = jax.random.split(jax.random.key(seed), 6)
    raw_traces = gaussian(seeds[0], (N_WIN, FILE_ROWS, L), 1.0, 6.0, ((0, 2), (1, 128)))
    fir_taps = gaussian(seeds[1], (TAPS,), TAPS ** -0.5, 0.5)
    source_slot = draw_source_slot(jax.random.fold_in(seeds[5], 71), 0)
    present = with_ends((jax.random.randint(seeds[3], (WINDOWS, S), 0, 10) < 9).astype(jnp.int32), jax.random.fold_in(seeds[3], 1), 0, 1)
    lag_start = with_ends(jax.random.randint(seeds[4], (S, S), 0 - L // 2, L // 2 - LAGW + 1), jax.random.fold_in(seeds[4], 1), 0 - L // 2, (L // 2 - LAGW + 1) - 1).astype(jnp.int32)
    return dict(raw_traces=raw_traces, fir_taps=fir_taps, source_slot=source_slot, present=present, lag_start=lag_start)


tile_len = 128
smooth_half = 4
floor_share = 0.25
spread_eps = 1e-06

def fir_matrix(fir_taps):
    half_taps = (TAPS - 1) // 2
    rows_in = jnp.arange(3 * tile_len, dtype=jnp.int32)[:, None]
    cols_out = jnp.arange(tile_len, dtype=jnp.int32)[None, :]
    offset = rows_in // tile_len - 1
    within = rows_in % tile_len
    tap_index = cols_out - within - offset * tile_len + half_taps
    inside = (tap_index >= 0) & (tap_index < TAPS)
    picked = fir_taps[jnp.clip(tap_index, 0, TAPS - 1)]
    return jnp.where(inside, picked, jnp.zeros((), fir_taps.dtype))

def dft_table():
    sample = jnp.arange(L, dtype=jnp.int32)[:, None]
    bins = BIN0 + jnp.arange(FB, dtype=jnp.int32)[None, :]
    angle = (sample * bins % L).astype(jnp.float32) * (2.0 * math.pi / L)
    return jnp.concatenate([jnp.cos(angle), -jnp.sin(angle)], axis=1).astype(jnp.bfloat16)

def whiten(traces, fir_taps):
    row_count = traces.shape[0]
    tiles = L // tile_len
    blocked = traces.reshape(row_count, tiles, tile_len)
    padded = jnp.pad(blocked, ((0, 0), (1, 1), (0, 0)))
    windowed = jnp.concatenate([padded[:, :-2], padded[:, 1:-1], padded[:, 2:]], axis=2)
    filtered = jnp.dot(windowed.reshape(row_count * tiles, 3 * tile_len), fir_matrix(fir_taps), preferred_element_type=jnp.float32)
    filtered = filtered.reshape(row_count, L).astype(jnp.bfloat16)
    spectrum = jnp.dot(filtered, dft_table(), preferred_element_type=jnp.float32)
    real_part = spectrum[:, :FB]
    imag_part = spectrum[:, FB:]
    magnitude = jnp.sqrt(real_part * real_part + imag_part * imag_part)
    padded_mag = jnp.pad(magnitude, ((0, 0), (smooth_half, smooth_half)))
    running = padded_mag[:, 0:FB]
    for shift_by in range(1, 2 * smooth_half + 1):
        running = running + padded_mag[:, shift_by:shift_by + FB]
    bins = jnp.arange(FB, dtype=jnp.int32)
    counts = (jnp.minimum(bins + smooth_half, FB - 1) - jnp.maximum(bins - smooth_half, 0) + 1).astype(jnp.float32)
    amplitude = running / counts[None, :]
    spread = jnp.sqrt(lax.optimization_barrier(jnp.mean(magnitude * magnitude, axis=1, keepdims=True)) + spread_eps)
    divisor = jnp.maximum(amplitude, floor_share * spread)
    return jnp.concatenate([real_part / divisor, imag_part / divisor], axis=1).astype(jnp.bfloat16)

def lag_transform(cross_sum, lag_first, scale_factor):
    bins = BIN0 + jnp.arange(FB, dtype=jnp.int32)
    phase_int = lag_first[..., None].astype(jnp.int32) * bins % L
    alpha_angle = phase_int.astype(jnp.float32) * (2.0 * math.pi / L)
    cos_alpha = jnp.cos(alpha_angle)
    sin_alpha = jnp.sin(alpha_angle)
    cross_re = cross_sum[..., :FB]
    cross_im = cross_sum[..., FB:]
    rotated = jnp.concatenate([cross_re * cos_alpha - cross_im * sin_alpha, cross_re * sin_alpha + cross_im * cos_alpha], axis=-1)
    lag_index = jnp.arange(LAGW, dtype=jnp.int32)
    beta_angle = (bins[:, None] * lag_index[None, :] % L).astype(jnp.float32) * (2.0 * math.pi / L)
    lag_table = jnp.concatenate([jnp.cos(beta_angle), -jnp.sin(beta_angle)], axis=0)
    flat_rows = rotated.reshape(-1, 2 * FB)
    lag_values = jnp.dot(flat_rows, lag_table, precision=lax.Precision.HIGHEST, preferred_element_type=jnp.float32)
    return (lag_values * scale_factor).reshape(cross_sum.shape[0], cross_sum.shape[1], LAGW)

def reference(raw_traces, fir_taps, source_slot, present, lag_start):
    flat_raw = raw_traces.reshape(N_WIN * FILE_ROWS, L)
    owners = jnp.arange(S, dtype=jnp.int32) // STD

    def per_window(window_index):
        shard_index = window_index // WDEV
        slot_row = source_slot[window_index]
        flat_row = shard_index * FILE_ROWS + slot_row // CAP * SLOTS + owners * CAP + slot_row % CAP
        traces = jnp.take(flat_raw, flat_row, axis=0)
        keep_mask = present[window_index][:, None].astype(jnp.bfloat16)
        return whiten(traces, fir_taps) * keep_mask
    spectra = lax.map(per_window, jnp.arange(WINDOWS, dtype=jnp.int32))
    widened = spectra.astype(jnp.float32)
    right_side = jnp.concatenate([widened[..., :FB], widened[..., FB:]], axis=1)
    scale_factor = 1.0 / math.sqrt(FB * WINDOWS)

    def per_block(block_index):
        own_rows = lax.dynamic_slice_in_dim(widened, block_index * STD, STD, 1)
        left_side = jnp.concatenate([own_rows[..., :FB], own_rows[..., FB:]], axis=1)
        product = jnp.einsum('wif,wjf->ijf', left_side, right_side, precision=lax.Precision.HIGHEST)
        real_part = product[:STD, :S] + product[STD:, S:]
        imag_part = product[STD:, :S] - product[:STD, S:]
        cross_sum = jnp.concatenate([real_part, imag_part], axis=2)
        lag_first = lax.dynamic_slice_in_dim(lag_start, block_index * STD, STD, 0)
        return lag_transform(cross_sum, lag_first, scale_factor)
    blocks = lax.map(per_block, jnp.arange(N_STA, dtype=jnp.int32))
    return blocks.reshape(S, S, LAGW)
```

```python
import functools
import math

import jax
import jax.numpy as jnp
import ml_dtypes
import numpy as np
from jax import lax
from jax.experimental import pallas as pl
from jax.experimental.pallas import tpu as pltpu
from jax.sharding import Mesh, PartitionSpec as P

L = 4096
TAPS = 127
FB = 64
BIN0 = 16
LAGW = 128
STD = 16
WDEV = 8
HALF = 1024

smooth_half = 4
floor_share = 0.25
spread_eps = 1e-06

column = np.arange(128)
column_bin = column // 16 * 8 + column % 8
column_im = column // 8 % 2

STA = ("ylo", "x", "z", "core")


def unit_angle(product):
    return ((product % L).astype(np.float32) * np.float32(2.0 * math.pi / L)).astype(np.float64)


def dft_table():
    angle = unit_angle(np.arange(L)[:, None] * (BIN0 + column_bin)[None, :])
    table = np.where(column_im == 0, np.cos(angle), -np.sin(angle))
    return table.astype(np.float32).astype(ml_dtypes.bfloat16)


def lag_table():
    angle = unit_angle((BIN0 + column_bin)[:, None] * np.arange(LAGW)[None, :])
    table = np.where(column_im[:, None] == 0, np.cos(angle), -np.sin(angle))
    return (table / math.sqrt(FB * 16)).astype(np.float32).astype(ml_dtypes.bfloat16)


def band_table():
    near = np.abs(column_bin[:, None] - column_bin[None, :]) <= smooth_half
    counts = (
        np.minimum(column_bin + smooth_half, FB - 1) - np.maximum(column_bin - smooth_half, 0) + 1
    )
    band = np.where(near & (column_im[:, None] == 0), 1.0, 0.0).astype(np.float32)
    return band, (1.0 / counts).astype(np.float32)[None, :]


def swap_parts(values):
    lane = lax.broadcasted_iota(jnp.int32, values.shape, 1)
    first = (lane // 8) % 2 == 0
    width = values.shape[1]
    return jnp.where(first, pltpu.roll(values, width - 8, 1), pltpu.roll(values, 8, 1))


def whiten_kernel(taps_ref, raw_ref, basis_ref, band_ref, inverse_ref, out_ref):
    taps = jnp.broadcast_to(taps_ref[...], (128, 512))
    chunks = []
    for chunk in range(4):
        first_shift = 128 * (chunk - 1) - 63
        moved = pltpu.roll(taps, first_shift % 512, 1, stride=1, stride_axis=0)
        chunks.append(moved[:, :256].astype(jnp.bfloat16))
    fir = jnp.concatenate(chunks, axis=0)
    spectrum = jnp.zeros((256, 128), jnp.float32)
    for tile in range(L // 256):
        first, last = 256 * tile - 128, 256 * tile + 384
        low, high = max(first, 0), min(last, L)
        filtered = jnp.dot(
            raw_ref[:, low:high],
            fir[low - first : 512 - (last - high)],
            preferred_element_type=jnp.float32,
        ).astype(jnp.bfloat16)
        spectrum += jnp.dot(
            filtered,
            basis_ref[256 * tile : 256 * (tile + 1), :],
            preferred_element_type=jnp.float32,
        )
    square = spectrum * spectrum
    magnitude = jnp.sqrt(square + swap_parts(square))
    amplitude = (
        jnp.dot(
            magnitude,
            band_ref[...],
            precision=lax.Precision.HIGHEST,
            preferred_element_type=jnp.float32,
        )
        * inverse_ref[...]
    )
    spread = jnp.sqrt(jnp.sum(square, axis=1, keepdims=True) * (1.0 / FB) + spread_eps)
    divisor = jnp.maximum(amplitude, floor_share * spread)
    out_ref[...] = (spectrum / divisor).astype(jnp.bfloat16)


def whiten(taps, raw):
    band, inverse = band_table()
    return pl.pallas_call(
        whiten_kernel,
        out_shape=jax.ShapeDtypeStruct((raw.shape[0], 128), jnp.bfloat16),
        compiler_params=pltpu.CompilerParams(vmem_limit_bytes=32 * 1024 * 1024),
        name="whiten",
    )(taps, raw, jnp.asarray(dft_table()), jnp.asarray(band), jnp.asarray(inverse))


def select_kernel(slot_ref, present_ref, rows_ref, out_ref):
    entry = lax.broadcasted_iota(jnp.int32, (128, 256), 1)
    selector = (slot_ref[...] == entry).astype(jnp.bfloat16)
    chosen = jnp.dot(selector, rows_ref[...], preferred_element_type=jnp.float32)
    chosen = chosen * present_ref[...].astype(jnp.float32)
    lane = lax.broadcasted_iota(jnp.int32, (STD, 128), 1) // 16
    for group in range(8):
        packed = jnp.zeros((STD, 128), jnp.float32)
        for window in range(WDEV):
            rows = chosen[window * STD : (window + 1) * STD]
            moved = pltpu.roll(rows, (window - group) * 16 % 128, 1) if window != group else rows
            packed = jnp.where(lane == window, moved, packed)
        out_ref[:, group * 128 : (group + 1) * 128] = packed.astype(jnp.bfloat16)


def select(slots, present, rows):
    return pl.pallas_call(
        select_kernel,
        out_shape=jax.ShapeDtypeStruct((STD, 1024), jnp.bfloat16),
        name="select",
    )(slots.reshape(-1, 1), present.reshape(-1, 1), rows)


cos_terms = (0.999999211, -19.7389804, 64.9286574, -85.2716215, 58.7904921, -21.0711056)
sin_terms = (6.28318492, -41.3415892, 81.5999433, -76.6144725, 41.3428824, -12.4712435)


def cos_sin(steps):
    turn = steps * (1.0 / L)
    turn = turn - jnp.round(turn)
    square = turn * turn
    cosine = jnp.full_like(square, cos_terms[-1])
    sine = jnp.full_like(square, sin_terms[-1])
    for cos_term, sin_term in zip(cos_terms[-2::-1], sin_terms[-2::-1]):
        cosine = cosine * square + cos_term
        sine = sine * square + sin_term
    return cosine, sine * turn


def correlate_kernel(piece_rows, place_ref, lag_ref, own_ref, table_ref, *rest):
    pieces = rest[: len(piece_rows)]
    out_ref, partners, weights, cross, sems = rest[len(piece_rows) :]
    step = pl.program_id(0)
    x, z, core = place_ref[0], place_ref[1], place_ref[2]

    def copy(number, source_x, target_x):
        first_x, _, z_back, core_back = piece_rows[number]
        z_at = lax.rem(z - z_back + 8, 8)
        core_at = lax.rem(core + core_back, 2)
        row = pl.multiple_of(z_at * 32 + core_at * 16, 16)
        return pltpu.make_async_copy(
            pieces[number].at[source_x - first_x],
            partners.at[target_x, :, pl.ds(row, 16), :],
            sems.at[target_x, z_back * 2 + core_back],
        )

    @pl.when(step == 0)
    def _():
        for number, (first_x, last_x, _, _) in enumerate(piece_rows):
            for source_x in range(first_x, last_x):
                copy(number, source_x, lax.rem(x - source_x + 4, 4)).start()
        own_lane = lax.broadcasted_iota(jnp.int32, (8, 256), 1)
        same_bin = own_lane % 8 == lax.broadcasted_iota(jnp.int32, (8, 256), 0)
        first = (lax.broadcasted_iota(jnp.int32, (STD, 256), 1) // 8) % 2 == 0
        for group in range(8):
            lanes = slice(group * 128, (group + 1) * 128)
            own = jnp.concatenate([own_ref[0, :, lanes], own_ref[1, :, lanes]], axis=1)
            own = own.astype(jnp.float32)
            swapped = swap_parts(own)
            swapped = jnp.where(first, swapped, -swapped)
            rows = []
            for station in range(STD):
                for part in (own, swapped):
                    row = jnp.broadcast_to(part[station : station + 1], (8, 256))
                    rows.append(jnp.where(same_bin, row, 0.0))
            weights[group] = jnp.concatenate(rows, axis=0).astype(jnp.bfloat16)

    seen = set()
    for number, (first_x, _, z_back, core_back) in enumerate(piece_rows):
        if (z_back, core_back) not in seen:
            seen.add((z_back, core_back))
            copy(number, first_x, step).wait()

    for group in range(8):
        lanes = slice(group * 128, (group + 1) * 128)
        partner = jnp.concatenate([partners[step, 0, :, lanes], partners[step, 1, :, lanes]], axis=1)
        cross[group] = lax.dot_general(
            weights[group], partner, (((1,), (1,)), ((), ())), preferred_element_type=jnp.float32
        )

    bins = (lax.broadcasted_iota(jnp.int32, (8, 128), 0) + BIN0).astype(jnp.float32)

    def one_station(station, carry):
        top = pl.multiple_of(station * 16, 16)
        for side in range(2):
            columns = slice(side * 128, (side + 1) * 128)
            lag = lag_ref[station, :, columns].astype(jnp.float32)
            lag = jnp.broadcast_to(lag, (8, 128))
            cosine, sine = cos_sin(lag * bins)
            cos_next, sin_next = cos_sin(lag * 8.0)
            rotated = []
            for group in range(8):
                real = cross[group, pl.ds(top, 8), columns]
                imag = cross[group, pl.ds(top + 8, 8), columns]
                rotated.append(real * cosine - imag * sine)
                rotated.append(real * sine + imag * cosine)
                if group < 7:
                    cosine, sine = (
                        cosine * cos_next - sine * sin_next,
                        cosine * sin_next + sine * cos_next,
                    )
            rotated = jnp.concatenate(rotated, axis=0).astype(jnp.bfloat16)
            out_ref[station, columns, :] = lax.dot_general(
                rotated,
                table_ref[...],
                (((0,), (0,)), ((), ())),
                preferred_element_type=jnp.float32,
            )
        return carry

    lax.fori_loop(0, STD, one_station, 0, unroll=4)


def correlate(place, lag, own, pieces, piece_rows):
    grid_spec = pltpu.PrefetchScalarGridSpec(
        num_scalar_prefetch=1,
        grid=(4,),
        in_specs=[
            pl.BlockSpec((STD, 1, 256), lambda q, place: (0, 0, q)),
            pl.BlockSpec((2, STD, 1024), lambda q, place: (0, 0, 0)),
            pl.BlockSpec((128, 128), lambda q, place: (0, 0)),
        ]
        + [pl.BlockSpec(memory_space=pl.ANY)] * len(pieces),
        out_specs=pl.BlockSpec((STD, 256, LAGW), lambda q, place: (0, q, 0)),
        scratch_shapes=[
            pltpu.VMEM((4, 2, 256, 1024), jnp.bfloat16),
            pltpu.VMEM((8, 256, 256), jnp.bfloat16),
            pltpu.VMEM((8, 256, 256), jnp.float32),
            pltpu.SemaphoreType.DMA((4, 16)),
        ],
    )
    return pl.pallas_call(
        functools.partial(correlate_kernel, piece_rows),
        grid_spec=grid_spec,
        out_shape=jax.ShapeDtypeStruct((STD, HALF, LAGW), jnp.float32),
        compiler_params=pltpu.CompilerParams(
            vmem_limit_bytes=40 * 1024 * 1024, dimension_semantics=("arbitrary",)
        ),
        name="correlate",
    )(place, lag.reshape(STD, 1, HALF), own, jnp.asarray(lag_table()), *pieces)


def shift(value, axis, size, by):
    return lax.ppermute(value, axis, [(at, (at + by) % size) for at in range(size)])


def per_device(raw_traces, fir_taps, source_slot, present, lag_start):
    ylo, yhi = lax.axis_index("ylo"), lax.axis_index("yhi")
    place = jnp.stack([lax.axis_index("x"), lax.axis_index("z"), lax.axis_index("core")])
    lag = lax.dynamic_slice_in_dim(lag_start, yhi * HALF, HALF, 1)

    taps = jnp.pad(fir_taps.astype(jnp.float32), (0, 512 - TAPS)).reshape(1, 512)
    white = whiten(taps, raw_traces[0])
    received = lax.all_to_all(white, STA, split_axis=0, concat_axis=0, tiled=True)
    mine = select(source_slot, present, received)

    ring = lax.ppermute(mine, ("ylo", "yhi"), [(0, 2), (2, 3), (3, 1), (1, 0)])
    middle = lax.ppermute(mine, ("ylo", "yhi"), [(1, 2), (2, 1)])
    other = shift(mine, "yhi", 2, 1)
    y = 2 * yhi + ylo
    early = jnp.where(y == 0, mine, jnp.where(y == 2, middle, ring))
    late = jnp.where(y == 3, mine, jnp.where(y == 1, middle, ring))
    own = jnp.stack([jnp.where(yhi == 0, mine, other), jnp.where(yhi == 0, other, mine)])

    block = jnp.stack([early, late])
    line = jnp.stack([block] + [shift(block, "x", 4, by) for by in (1, 2, 3)])
    pieces, piece_rows = [line], [(0, 4, 0)]
    up = down = line
    for hop in (1, 2, 3):
        up, down = shift(up, "z", 8, 1), shift(down, "z", 8, -1)
        pieces += [up, down]
        piece_rows += [(0, 4, hop), (0, 4, 8 - hop)]
    pieces += [shift(up[:2], "z", 8, 1), shift(down[2:], "z", 8, -1)]
    piece_rows += [(0, 2, 4), (2, 4, 4)]
    theirs = [shift(piece, "core", 2, 1) for piece in pieces]
    rows = tuple(row + (0,) for row in piece_rows) + tuple(row + (1,) for row in piece_rows)
    return correlate(place, lag, own, pieces + theirs, rows)


def solution(mesh):
    fine = Mesh(mesh.devices.reshape(2, 4, 8, 2, 2), STA + ("yhi",))
    placed = (P("yhi", STA, None), P(), P("yhi", STA), P("yhi", STA), P(STA, None))
    return jax.shard_map(
        per_device, mesh=fine, in_specs=placed, out_specs=P(STA, "yhi", None), check_vma=False
    )
```

```python
import functools
import math

import jax
import jax.numpy as jnp
import ml_dtypes
import numpy as np
from jax import lax
from jax.experimental import pallas as pl
from jax.experimental.pallas import tpu as pltpu
from jax.sharding import Mesh, PartitionSpec as P

L = 4096
TAPS = 127
FB = 64
BIN0 = 16
LAGW = 128
STD = 16
WDEV = 8
HALF = 1024

smooth_half = 4
floor_share = 0.25
spread_eps = 1e-06

column = np.arange(128)
column_bin = column // 16 * 8 + column % 8
column_im = column // 8 % 2

STA = ("ylo", "x", "z", "core")


def unit_angle(product):
    return ((product % L).astype(np.float32) * np.float32(2.0 * math.pi / L)).astype(np.float64)


def dft_table():
    angle = unit_angle(np.arange(L)[:, None] * (BIN0 + column_bin)[None, :])
    table = np.where(column_im == 0, np.cos(angle), -np.sin(angle))
    return table.astype(np.float32).astype(ml_dtypes.bfloat16)


def lag_table():
    angle = unit_angle((BIN0 + column_bin)[:, None] * np.arange(LAGW)[None, :])
    table = np.where(column_im[:, None] == 0, np.cos(angle), -np.sin(angle))
    return (table / math.sqrt(FB * 16)).astype(np.float32).astype(ml_dtypes.bfloat16)


def band_table():
    near = np.abs(column_bin[:, None] - column_bin[None, :]) <= smooth_half
    counts = (
        np.minimum(column_bin + smooth_half, FB - 1) - np.maximum(column_bin - smooth_half, 0) + 1
    )
    band = np.where(near & (column_im[:, None] == 0), 1.0, 0.0).astype(np.float32)
    return band, (1.0 / counts).astype(np.float32)[None, :]


def swap_parts(values):
    lane = lax.broadcasted_iota(jnp.int32, values.shape, 1)
    first = (lane // 8) % 2 == 0
    width = values.shape[1]
    return jnp.where(first, pltpu.roll(values, width - 8, 1), pltpu.roll(values, 8, 1))


def whiten_kernel(taps_ref, raw_hbm, basis_hbm, band_ref, inverse_ref, out_ref, raw_ref, basis_ref, wide, sems):
    raw_copies = []
    for chunk in range(4):
        columns = slice(chunk * 1024, (chunk + 1) * 1024)
        raw_copies.append(
            pltpu.make_async_copy(raw_hbm.at[:, columns], raw_ref.at[:, columns], sems.at[chunk])
        )
    basis_copy = pltpu.make_async_copy(basis_hbm, basis_ref, sems.at[4])
    raw_copies[0].start()
    raw_copies[1].start()
    basis_copy.start()
    raw_copies[2].start()
    raw_copies[3].start()

    wide[...] = jnp.zeros((1, 512), jnp.float32)
    wide[:, :TAPS] = taps_ref[...].astype(jnp.float32)
    taps = jnp.broadcast_to(wide[...], (128, 512))
    chunks = []
    for chunk in range(4):
        first_shift = 128 * (chunk - 1) - 63
        moved = pltpu.roll(taps, first_shift % 512, 1, stride=1, stride_axis=0)
        chunks.append(moved[:, :256].astype(jnp.bfloat16))
    fir = jnp.concatenate(chunks, axis=0)
    spectrum = jnp.zeros((256, 128), jnp.float32)
    arrived = 0
    for tile in range(L // 256):
        first, last = 256 * tile - 128, 256 * tile + 384
        low, high = max(first, 0), min(last, L)
        while arrived * 1024 < high:
            raw_copies[arrived].wait()
            arrived += 1
        if tile == 0:
            basis_copy.wait()
        filtered = jnp.dot(
            raw_ref[:, low:high],
            fir[low - first : 512 - (last - high)],
            preferred_element_type=jnp.float32,
        ).astype(jnp.bfloat16)
        spectrum += jnp.dot(
            filtered,
            basis_ref[256 * tile : 256 * (tile + 1), :],
            preferred_element_type=jnp.float32,
        )
    square = spectrum * spectrum
    magnitude = jnp.sqrt(square + swap_parts(square))
    amplitude = (
        jnp.dot(
            magnitude,
            band_ref[...],
            precision=lax.Precision.HIGHEST,
            preferred_element_type=jnp.float32,
        )
        * inverse_ref[...]
    )
    spread = jnp.sqrt(jnp.sum(square, axis=1, keepdims=True) * (1.0 / FB) + spread_eps)
    divisor = jnp.maximum(amplitude, floor_share * spread)
    out_ref[...] = (spectrum / divisor).astype(jnp.bfloat16)


def whiten(taps, raw):
    band, inverse = band_table()
    return pl.pallas_call(
        whiten_kernel,
        out_shape=jax.ShapeDtypeStruct((256, 128), jnp.bfloat16),
        in_specs=[
            pl.BlockSpec(memory_space=pltpu.VMEM),
            pl.BlockSpec(memory_space=pl.ANY),
            pl.BlockSpec(memory_space=pl.ANY),
            pl.BlockSpec(memory_space=pltpu.VMEM),
            pl.BlockSpec(memory_space=pltpu.VMEM),
        ],
        scratch_shapes=[
            pltpu.VMEM((256, L), jnp.bfloat16),
            pltpu.VMEM((L, 128), jnp.bfloat16),
            pltpu.VMEM((1, 512), jnp.float32),
            pltpu.SemaphoreType.DMA((5,)),
        ],
        compiler_params=pltpu.CompilerParams(vmem_limit_bytes=56 * 1024 * 1024),
        name="whiten",
    )(taps, raw, jnp.asarray(dft_table()), jnp.asarray(band), jnp.asarray(inverse))


def select_kernel(slot_ref, present_ref, rows_ref, out_ref):
    entry = lax.broadcasted_iota(jnp.int32, (128, 256), 1)
    selector = (slot_ref[...] == entry).astype(jnp.bfloat16)
    chosen = jnp.dot(selector, rows_ref[...], preferred_element_type=jnp.float32)
    chosen = chosen * present_ref[...].astype(jnp.float32)
    lane = lax.broadcasted_iota(jnp.int32, (STD, 128), 1) // 16
    for group in range(8):
        packed = jnp.zeros((STD, 128), jnp.float32)
        for window in range(WDEV):
            rows = chosen[window * STD : (window + 1) * STD]
            moved = pltpu.roll(rows, (window - group) * 16 % 128, 1) if window != group else rows
            packed = jnp.where(lane == window, moved, packed)
        out_ref[:, group * 128 : (group + 1) * 128] = packed.astype(jnp.bfloat16)


def select(slots, present, rows):
    return pl.pallas_call(
        select_kernel,
        out_shape=jax.ShapeDtypeStruct((STD, 1024), jnp.bfloat16),
        name="select",
    )(slots.reshape(-1, 1), present.reshape(-1, 1), rows)


cos_terms = (0.999999211, -19.7389804, 64.9286574, -85.2716215, 58.7904921, -21.0711056)
sin_terms = (6.28318492, -41.3415892, 81.5999433, -76.6144725, 41.3428824, -12.4712435)


def cos_sin(steps):
    turn = steps * (1.0 / L)
    turn = turn - jnp.round(turn)
    square = turn * turn
    cosine = jnp.full_like(square, cos_terms[-1])
    sine = jnp.full_like(square, sin_terms[-1])
    for cos_term, sin_term in zip(cos_terms[-2::-1], sin_terms[-2::-1]):
        cosine = cosine * square + cos_term
        sine = sine * square + sin_term
    return cosine, sine * turn


def phase_kernel(place_ref, lag_ref, out_ref):
    x, core = place_ref[0], place_ref[1]
    lane = lax.broadcasted_iota(jnp.int32, (STD, 128), 1)
    bins = (lax.broadcasted_iota(jnp.int32, (8, 128), 0) + BIN0).astype(jnp.float32)
    for z in range(8):
        tile = jnp.zeros((STD, 128), jnp.int32)
        for x_at in range(4):
            first = (x_at * 256 + z * 32) // 128 * 128
            part = lag_ref[:, first : first + 128]
            by = (x_at - z % 4) * 32 % 128
            tile = jnp.where(lane // 32 == x_at, pltpu.roll(part, by, 1) if by else part, tile)
        tile = pltpu.roll(tile, lax.rem(128 - 32 * x, 128), 1)
        crossed = jnp.where((lane // 16) % 2 == 0, pltpu.roll(tile, 112, 1), pltpu.roll(tile, 16, 1))
        lag = jnp.where(core == 1, crossed, tile).astype(jnp.float32)
        out_ref[z, 256:272, :], out_ref[z, 272:288, :] = cos_sin(lag * 8.0)
        for station in range(STD):
            low, high = station * 8, station * 8 + 8
            steps = jnp.broadcast_to(lag[station : station + 1], (8, 128)) * bins
            out_ref[z, low:high, :], out_ref[z, 128 + low : 128 + high, :] = cos_sin(steps)


def phases(place, lag):
    return pl.pallas_call(
        phase_kernel,
        in_specs=[pl.BlockSpec(memory_space=pltpu.SMEM), pl.BlockSpec(memory_space=pltpu.VMEM)],
        out_shape=jax.ShapeDtypeStruct((8, 288, 128), jnp.float32),
        cost_estimate=pl.CostEstimate(flops=1 << 20, bytes_accessed=1 << 16, transcendentals=0),
        name="phases",
    )(place, lag)


def weight_kernel(yhi_ref, mine_ref, other_ref, table_ref, out_ref):
    out_ref[8, :128, :128] = table_ref[...]
    mine_first = yhi_ref[0] == 0
    own_lane = lax.broadcasted_iota(jnp.int32, (8, 256), 1)
    same_bin = own_lane % 8 == lax.broadcasted_iota(jnp.int32, (8, 256), 0)
    first = (lax.broadcasted_iota(jnp.int32, (STD, 256), 1) // 8) % 2 == 0
    for group in range(8):
        lanes = slice(group * 128, (group + 1) * 128)
        mine = mine_ref[:, lanes].astype(jnp.float32)
        other = other_ref[:, lanes].astype(jnp.float32)
        early = jnp.where(mine_first, mine, other)
        own = jnp.concatenate([early, jnp.where(mine_first, other, mine)], axis=1)
        swapped = swap_parts(own)
        swapped = jnp.where(first, swapped, -swapped)
        rows = []
        for station in range(STD):
            for part in (own, swapped):
                row = jnp.broadcast_to(part[station : station + 1], (8, 256))
                rows.append(jnp.where(same_bin, row, 0.0))
        out_ref[group] = jnp.concatenate(rows, axis=0).astype(jnp.bfloat16)


def pair_weights(yhi, mine, other):
    return pl.pallas_call(
        weight_kernel,
        in_specs=[
            pl.BlockSpec(memory_space=pltpu.SMEM),
            pl.BlockSpec(memory_space=pltpu.VMEM),
            pl.BlockSpec(memory_space=pltpu.VMEM),
            pl.BlockSpec(memory_space=pltpu.VMEM),
        ],
        out_shape=jax.ShapeDtypeStruct((9, 256, 256), jnp.bfloat16),
        cost_estimate=pl.CostEstimate(flops=1 << 20, bytes_accessed=1 << 16, transcendentals=0),
        name="pair_weights",
    )(yhi, mine, other, jnp.asarray(lag_table()))


def correlate_kernel(layout, place_ref, weight_ref, turn_ref, *rest):
    count = sum(len(parts) for parts in layout)
    mine, theirs = rest[:count], rest[count : 2 * count]
    out_ref, cross = rest[-2:]
    step = pl.program_id(0)
    x, core = place_ref[0], place_ref[1]

    @pl.when(step == 0)
    def _():
        for group in range(8):
            lanes = slice(group * 128, (group + 1) * 128)
            halves = []
            for half in range(2):
                blocks = []
                for parts in layout:
                    for number, rows in parts:
                        for row in range(rows):
                            blocks.append(mine[number][row, half, :, lanes])
                            blocks.append(theirs[number][row, half, :, lanes])
                halves.append(jnp.concatenate(blocks, axis=0))
            product = lax.dot_general(
                weight_ref[group],
                jnp.concatenate(halves, axis=1),
                (((1,), (1,)), ((), ())),
                preferred_element_type=jnp.float32,
            )
            for at in range(len(layout)):
                cross[at, group] = product[:, at * 128 : (at + 1) * 128]

    for station in range(STD):
        top = station * 16
        cosine = turn_ref[0, station * 8 : station * 8 + 8, :]
        sine = turn_ref[0, station * 8 + 128 : station * 8 + 136, :]
        cos_next = jnp.broadcast_to(turn_ref[0, station + 256 : station + 257, :], (8, 128))
        sin_next = jnp.broadcast_to(turn_ref[0, station + 272 : station + 273, :], (8, 128))
        rotated = []
        for group in range(8):
            real = cross[step, group, top : top + 8, :]
            imag = cross[step, group, top + 8 : top + 16, :]
            rotated.append(real * cosine - imag * sine)
            rotated.append(real * sine + imag * cosine)
            if group < 7:
                cosine, sine = (
                    cosine * cos_next - sine * sin_next,
                    cosine * sin_next + sine * cos_next,
                )
        rotated = jnp.concatenate(rotated, axis=0).astype(jnp.bfloat16)
        values = lax.dot_general(
            rotated, weight_ref[8, :128, :128], (((0,), (0,)), ((), ())), preferred_element_type=jnp.float32
        )
        for ahead in range(4):
            for other in range(2):
                row = pl.multiple_of(lax.rem(core + other, 2) * 16, 16)
                first = ahead * 32 + other * 16
                out_ref[station, lax.rem(x + ahead, 4), 0, pl.ds(row, 16), :] = values[
                    first : first + 16
                ]


def correlate(place, weights, turns, previous, hop, mine, theirs):
    cost = (1 << 31, 1 << 30, 1 << 28, 1 << 31, 1 << 30)[hop]
    layout, number = [], 0
    for parts in mine:
        layout.append([])
        for part in parts:
            layout[-1].append((number, part.shape[0]))
            number += 1
    steps = len(layout)

    def z_at(step, place):
        return lax.rem(place[2] + (8 - hop) + step * (2 * hop - 8), 8)

    whole = lambda shape: pl.BlockSpec(shape, lambda step, place: (0,) * len(shape))
    blocks = [part for parts in mine for part in parts] + [part for parts in theirs for part in parts]
    operands = [place, weights, turns, *blocks]
    in_specs = [whole((9, 256, 256))]
    in_specs += [pl.BlockSpec((1, 288, 128), lambda step, place: (z_at(step, place), 0, 0))]
    in_specs += [whole(block.shape) for block in blocks]
    aliases = {}
    if previous is not None:
        aliases = {len(operands): 0}
        operands.append(previous)
        in_specs.append(pl.BlockSpec(memory_space=pl.ANY))
    return pl.pallas_call(
        functools.partial(correlate_kernel, layout),
        grid_spec=pltpu.PrefetchScalarGridSpec(
            num_scalar_prefetch=1,
            grid=(steps,),
            in_specs=in_specs,
            out_specs=pl.BlockSpec(
                (STD, 4, 1, 32, LAGW), lambda step, place: (0, 0, z_at(step, place), 0, 0)
            ),
            scratch_shapes=[pltpu.VMEM((steps, 8, 256, 128), jnp.float32)],
        ),
        out_shape=jax.ShapeDtypeStruct((STD, 4, 8, 32, LAGW), jnp.float32),
        input_output_aliases=aliases,
        compiler_params=pltpu.CompilerParams(
            vmem_limit_bytes=24 * 1024 * 1024, dimension_semantics=("arbitrary",)
        ),
        cost_estimate=pl.CostEstimate(
            flops=cost, bytes_accessed=1 << 16, transcendentals=0
        ),
        name="correlate",
    )(*operands)


def shift(value, axis, size, by):
    return lax.ppermute(value, axis, [(at, (at + by) % size) for at in range(size)])


def per_device(raw_traces, fir_taps, source_slot, present, lag_start):
    ylo, yhi = lax.axis_index("ylo"), lax.axis_index("yhi")
    place = jnp.stack([lax.axis_index("x"), lax.axis_index("core"), lax.axis_index("z")])
    lag = lax.dynamic_slice_in_dim(lag_start, yhi * HALF, HALF, 1)
    white = whiten(fir_taps.reshape(1, TAPS), raw_traces[0])
    white, lag = lax.optimization_barrier((white, lag))
    received = lax.all_to_all(white, STA, split_axis=0, concat_axis=0, tiled=True)
    received, place, turns = lax.optimization_barrier((received, place, phases(place, lag)))
    mine = select(source_slot, present, received)

    ring = lax.ppermute(mine, ("ylo", "yhi"), [(0, 2), (2, 3), (3, 1), (1, 0)])
    middle = lax.ppermute(mine, ("ylo", "yhi"), [(1, 2), (2, 1)])
    y = 2 * yhi + ylo
    early = jnp.where(y == 0, mine, jnp.where(y == 2, middle, ring))
    late = jnp.where(y == 3, mine, jnp.where(y == 1, middle, ring))
    block = jnp.stack([early, late])
    block, mine = lax.optimization_barrier((block, mine))
    other = shift(mine, "yhi", 2, 1)
    blocks = [block] + [shift(block, "x", 4, -by) for by in (1, 2, 3)]
    blocks, other = lax.optimization_barrier((blocks, other))
    line = jnp.stack(blocks)
    weights = pair_weights(yhi.reshape(1), mine, other)

    across = lambda value: shift(value, "core", 2, 1)
    up = down = line
    hops = [[[line]]]
    for _ in range(3):
        up, down = shift(up, "z", 8, 1), shift(down, "z", 8, -1)
        hops.append([[up], [down]])
    hops.append([[shift(up[:2], "z", 8, 1), shift(down[2:], "z", 8, -1)]])
    out = None
    for hop, mine_here in enumerate(hops):
        ready = mine_here
        if hop in (1, 2):
            ready, out = lax.optimization_barrier((mine_here, out))
        theirs = [[across(part) for part in parts] for parts in ready]
        out = correlate(place, weights, turns, out, hop, mine_here, theirs)
    return out.reshape(STD, HALF, LAGW)


def solution(mesh):
    fine = Mesh(mesh.devices.reshape(2, 4, 8, 2, 2), STA + ("yhi",))
    placed = (P("yhi", STA, None), P(), P("yhi", STA), P("yhi", STA), P(STA, None))
    return jax.shard_map(
        per_device, mesh=fine, in_specs=placed, out_specs=P(STA, "yhi", None), check_vma=False
    )
```

```python
import functools
import math

import jax
import jax.numpy as jnp
import ml_dtypes
import numpy as np
from jax import lax
from jax.experimental import pallas as pl
from jax.experimental.pallas import tpu as pltpu
from jax.sharding import Mesh, PartitionSpec as P

L = 4096
TAPS = 127
FB = 64
BIN0 = 16
LAGW = 128
STD = 16
WDEV = 8
HALF = 1024

smooth_half = 4
floor_share = 0.25
spread_eps = 1e-06

column = np.arange(128)
column_bin = column // 16 * 8 + column % 8
column_im = column // 8 % 2

STA = ("ylo", "x", "z", "core")


def unit_angle(product):
    return ((product % L).astype(np.float32) * np.float32(2.0 * math.pi / L)).astype(np.float64)


def dft_table():
    angle = unit_angle(np.arange(L)[:, None] * (BIN0 + column_bin)[None, :])
    table = np.where(column_im == 0, np.cos(angle), -np.sin(angle))
    return table.astype(np.float32).astype(ml_dtypes.bfloat16)


def lag_table():
    angle = unit_angle((BIN0 + column_bin)[:, None] * np.arange(LAGW)[None, :])
    table = np.where(column_im[:, None] == 0, np.cos(angle), -np.sin(angle))
    return (table / math.sqrt(FB * 16)).astype(np.float32).astype(ml_dtypes.bfloat16)


def band_table():
    near = np.abs(column_bin[:, None] - column_bin[None, :]) <= smooth_half
    counts = (
        np.minimum(column_bin + smooth_half, FB - 1) - np.maximum(column_bin - smooth_half, 0) + 1
    )
    band = np.where(near & (column_im[:, None] == 0), 1.0, 0.0).astype(np.float32)
    return band, (1.0 / counts).astype(np.float32)[None, :]


def swap_parts(values):
    lane = lax.broadcasted_iota(jnp.int32, values.shape, 1)
    first = (lane // 8) % 2 == 0
    width = values.shape[1]
    return jnp.where(first, pltpu.roll(values, width - 8, 1), pltpu.roll(values, 8, 1))


def whiten_kernel(taps_ref, raw_hbm, basis_hbm, band_ref, inverse_ref, out_ref, raw_ref, basis_ref, wide, sems):
    raw_copies = []
    for chunk in range(8):
        columns = slice(chunk * 512, (chunk + 1) * 512)
        raw_copies.append(
            pltpu.make_async_copy(raw_hbm.at[:, columns], raw_ref.at[:, columns], sems.at[chunk])
        )
    basis_copy = pltpu.make_async_copy(basis_hbm, basis_ref, sems.at[8])
    for chunk, raw_copy in enumerate(raw_copies):
        raw_copy.start()
        if chunk == 3:
            basis_copy.start()

    wide[...] = jnp.zeros((1, 512), jnp.float32)
    wide[:, :TAPS] = taps_ref[...].astype(jnp.float32)
    taps = jnp.broadcast_to(wide[...], (128, 512))
    chunks = []
    for chunk in range(4):
        first_shift = 128 * (chunk - 1) - 63
        moved = pltpu.roll(taps, first_shift % 512, 1, stride=1, stride_axis=0)
        chunks.append(moved[:, :256].astype(jnp.bfloat16))
    fir = jnp.concatenate(chunks, axis=0)
    fir_halves = fir[:256], fir[256:]
    edge = jnp.zeros((256, 128), jnp.bfloat16)
    spectrum = jnp.zeros((256, 128), jnp.float32)
    arrived = 0
    for group in range(4):
        tiles = range(group * 4, (group + 1) * 4)
        while arrived < 8 and arrived * 512 < tiles[-1] * 256 + 384:
            raw_copies[arrived].wait()
            arrived += 1
        filtered = jnp.zeros((256 * 4, 256), jnp.float32)
        for half in range(2):
            parts = []
            for tile in tiles:
                low = 256 * tile - 128 + 256 * half
                if low < 0:
                    parts.append(jnp.concatenate([edge, raw_ref[:, :128]], axis=1))
                elif low + 256 > L:
                    parts.append(jnp.concatenate([raw_ref[:, low:], edge], axis=1))
                else:
                    parts.append(raw_ref[:, low : low + 256])
            filtered += jnp.dot(
                jnp.concatenate(parts, axis=0),
                fir_halves[half],
                preferred_element_type=jnp.float32,
            )
        filtered = filtered.astype(jnp.bfloat16)
        if group == 0:
            basis_copy.wait()
        for number, tile in enumerate(tiles):
            spectrum += jnp.dot(
                filtered[256 * number : 256 * (number + 1)],
                basis_ref[256 * tile : 256 * (tile + 1), :],
                preferred_element_type=jnp.float32,
            )
    square = spectrum * spectrum
    magnitude = jnp.sqrt(square + swap_parts(square))
    amplitude = (
        jnp.dot(
            magnitude,
            band_ref[...],
            precision=lax.Precision.HIGHEST,
            preferred_element_type=jnp.float32,
        )
        * inverse_ref[...]
    )
    spread = jnp.sqrt(jnp.sum(square, axis=1, keepdims=True) * (1.0 / FB) + spread_eps)
    divisor = jnp.maximum(amplitude, floor_share * spread)
    out_ref[...] = (spectrum / divisor).astype(jnp.bfloat16)


def whiten(taps, raw):
    band, inverse = band_table()
    return pl.pallas_call(
        whiten_kernel,
        out_shape=jax.ShapeDtypeStruct((256, 128), jnp.bfloat16),
        in_specs=[
            pl.BlockSpec(memory_space=pltpu.VMEM),
            pl.BlockSpec(memory_space=pl.ANY),
            pl.BlockSpec(memory_space=pl.ANY),
            pl.BlockSpec(memory_space=pltpu.VMEM),
            pl.BlockSpec(memory_space=pltpu.VMEM),
        ],
        scratch_shapes=[
            pltpu.VMEM((256, L), jnp.bfloat16),
            pltpu.VMEM((L, 128), jnp.bfloat16),
            pltpu.VMEM((1, 512), jnp.float32),
            pltpu.SemaphoreType.DMA((9,)),
        ],
        compiler_params=pltpu.CompilerParams(vmem_limit_bytes=56 * 1024 * 1024),
        name="whiten",
    )(taps, raw, jnp.asarray(dft_table()), jnp.asarray(band), jnp.asarray(inverse))


def select_kernel(slot_ref, rows_ref, out_ref):
    slots = slot_ref[...]
    entry = lax.broadcasted_iota(jnp.int32, (256, STD), 0)
    stored = rows_ref[...]
    chosen = []
    for window in range(WDEV):
        picked = jnp.where(entry == slots[window : window + 1, :], 1.0, 0.0).astype(jnp.bfloat16)
        chosen.append(
            lax.dot_general(
                picked, stored, (((0,), (0,)), ((), ())), preferred_element_type=jnp.float32
            )
        )
    lane = lax.broadcasted_iota(jnp.int32, (STD, 128), 1) // 16
    for group in range(8):
        packed = jnp.zeros((STD, 128), jnp.float32)
        for window in range(WDEV):
            rows = chosen[window]
            moved = pltpu.roll(rows, (window - group) * 16 % 128, 1) if window != group else rows
            packed = jnp.where(lane == window, moved, packed)
        out_ref[:, group * 128 : (group + 1) * 128] = packed.astype(jnp.bfloat16)


def select(slots, rows):
    return pl.pallas_call(
        select_kernel,
        out_shape=jax.ShapeDtypeStruct((STD, 1024), jnp.bfloat16),
        compiler_params=pltpu.CompilerParams(vmem_limit_bytes=4 * 1024 * 1024),
        name="select",
    )(slots, rows)


cos_terms = (0.999999211, -19.7389804, 64.9286574, -85.2716215, 58.7904921, -21.0711056)
sin_terms = (6.28318492, -41.3415892, 81.5999433, -76.6144725, 41.3428824, -12.4712435)


def cos_sin(steps):
    turn = steps * (1.0 / L)
    turn = turn - jnp.round(turn)
    square = turn * turn
    cosine = jnp.full_like(square, cos_terms[-1])
    sine = jnp.full_like(square, sin_terms[-1])
    for cos_term, sin_term in zip(cos_terms[-2::-1], sin_terms[-2::-1]):
        cosine = cosine * square + cos_term
        sine = sine * square + sin_term
    return cosine, sine * turn


def phase_kernel(place_ref, lag_ref, table_ref, out_ref, table_out_ref):
    table_out_ref[...] = table_ref[...]
    x, core = place_ref[0], place_ref[1]
    lane = lax.broadcasted_iota(jnp.int32, (STD, 128), 1)
    bins = (lax.broadcasted_iota(jnp.int32, (8, 128), 0) + BIN0).astype(jnp.float32)
    for z in range(8):
        tile = jnp.zeros((STD, 128), jnp.int32)
        for x_at in range(4):
            first = (x_at * 256 + z * 32) // 128 * 128
            part = lag_ref[:, first : first + 128]
            by = (x_at - z % 4) * 32 % 128
            tile = jnp.where(lane // 32 == x_at, pltpu.roll(part, by, 1) if by else part, tile)
        tile = pltpu.roll(tile, lax.rem(128 - 32 * x, 128), 1)
        crossed = jnp.where((lane // 16) % 2 == 0, pltpu.roll(tile, 112, 1), pltpu.roll(tile, 16, 1))
        lag = jnp.where(core == 1, crossed, tile).astype(jnp.float32)
        out_ref[z, 256:272, :], out_ref[z, 272:288, :] = cos_sin(lag * 8.0)
        for station in range(STD):
            low, high = station * 8, station * 8 + 8
            steps = jnp.broadcast_to(lag[station : station + 1], (8, 128)) * bins
            out_ref[z, low:high, :], out_ref[z, 128 + low : 128 + high, :] = cos_sin(steps)


def phases(place, lag):
    return pl.pallas_call(
        phase_kernel,
        grid_spec=pltpu.PrefetchScalarGridSpec(
            num_scalar_prefetch=1,
            grid=(1,),
            in_specs=[
                pl.BlockSpec((STD, HALF), lambda step, place: (0, place[3])),
                pl.BlockSpec((128, 128), lambda step, place: (0, 0)),
            ],
            out_specs=[
                pl.BlockSpec((8, 288, 128), lambda step, place: (0, 0, 0)),
                pl.BlockSpec((128, 128), lambda step, place: (0, 0)),
            ],
        ),
        compiler_params=pltpu.CompilerParams(vmem_limit_bytes=8 * 1024 * 1024),
        out_shape=[
            jax.ShapeDtypeStruct((8, 288, 128), jnp.float32),
            jax.ShapeDtypeStruct((128, 128), jnp.bfloat16),
        ],
        cost_estimate=pl.CostEstimate(flops=1 << 20, bytes_accessed=1 << 16, transcendentals=0),
        name="phases",
    )(place, lag, jnp.asarray(lag_table()))


def weight_kernel(yhi_ref, mine_ref, other_ref, out_ref):
    mine_first = yhi_ref[0] == 0
    own_lane = lax.broadcasted_iota(jnp.int32, (8, 256), 1)
    same_bin = own_lane % 8 == lax.broadcasted_iota(jnp.int32, (8, 256), 0)
    first = (lax.broadcasted_iota(jnp.int32, (STD, 256), 1) // 8) % 2 == 0
    for group in range(8):
        lanes = slice(group * 128, (group + 1) * 128)
        mine = mine_ref[:, lanes].astype(jnp.float32)
        other = other_ref[:, lanes].astype(jnp.float32)
        early = jnp.where(mine_first, mine, other)
        own = jnp.concatenate([early, jnp.where(mine_first, other, mine)], axis=1)
        swapped = swap_parts(own)
        swapped = jnp.where(first, swapped, -swapped)
        rows = []
        for station in range(STD):
            for part in (own, swapped):
                row = jnp.broadcast_to(part[station : station + 1], (8, 256))
                rows.append(jnp.where(same_bin, row, 0.0))
        out_ref[group] = jnp.concatenate(rows, axis=0).astype(jnp.bfloat16)


def pair_weights(yhi, mine, other):
    return pl.pallas_call(
        weight_kernel,
        in_specs=[
            pl.BlockSpec(memory_space=pltpu.SMEM),
            pl.BlockSpec(memory_space=pltpu.VMEM),
            pl.BlockSpec(memory_space=pltpu.VMEM),
        ],
        out_shape=jax.ShapeDtypeStruct((8, 256, 256), jnp.bfloat16),
        compiler_params=pltpu.CompilerParams(vmem_limit_bytes=8 * 1024 * 1024),
        cost_estimate=pl.CostEstimate(flops=1 << 20, bytes_accessed=1 << 16, transcendentals=0),
        name="pair_weights",
    )(yhi, mine, other)


def correlate_kernel(layout, place_ref, weight_ref, table_ref, turn_ref, *rest):
    count = sum(len(parts) for parts in layout)
    mine, theirs = rest[:count], rest[count : 2 * count]
    out_ref, cross = rest[-2:]
    step = pl.program_id(0)
    x, core = place_ref[0], place_ref[1]

    @pl.when(step == 0)
    def _():
        for group in range(8):
            lanes = slice(group * 128, (group + 1) * 128)
            halves = []
            for half in range(2):
                blocks = []
                for parts in layout:
                    for number, rows in parts:
                        for row in range(rows):
                            blocks.append(mine[number][row, half, :, lanes])
                            blocks.append(theirs[number][row, half, :, lanes])
                halves.append(jnp.concatenate(blocks, axis=0))
            product = lax.dot_general(
                weight_ref[group],
                jnp.concatenate(halves, axis=1),
                (((1,), (1,)), ((), ())),
                preferred_element_type=jnp.float32,
            )
            for at in range(len(layout)):
                cross[at, group] = product[:, at * 128 : (at + 1) * 128]

    for station in range(STD):
        top = station * 16
        cosine = turn_ref[0, station * 8 : station * 8 + 8, :]
        sine = turn_ref[0, station * 8 + 128 : station * 8 + 136, :]
        cos_next = jnp.broadcast_to(turn_ref[0, station + 256 : station + 257, :], (8, 128))
        sin_next = jnp.broadcast_to(turn_ref[0, station + 272 : station + 273, :], (8, 128))
        rotated = []
        for group in range(8):
            real = cross[step, group, top : top + 8, :]
            imag = cross[step, group, top + 8 : top + 16, :]
            rotated.append(real * cosine - imag * sine)
            rotated.append(real * sine + imag * cosine)
            if group < 7:
                cosine, sine = (
                    cosine * cos_next - sine * sin_next,
                    cosine * sin_next + sine * cos_next,
                )
        rotated = jnp.concatenate(rotated, axis=0).astype(jnp.bfloat16)
        values = lax.dot_general(
            rotated, table_ref[...], (((0,), (0,)), ((), ())), preferred_element_type=jnp.float32
        )
        for ahead in range(4):
            for other in range(2):
                row = pl.multiple_of(lax.rem(core + other, 2) * 16, 16)
                first = ahead * 32 + other * 16
                out_ref[station, lax.rem(x + ahead, 4), 0, pl.ds(row, 16), :] = values[
                    first : first + 16
                ]


def correlate(place, weights, table, turns, previous, hop, mine, theirs):
    cost = (1 << 31, 1 << 30, 1 << 28, 1 << 31, 1 << 30)[hop]
    layout, number = [], 0
    for parts in mine:
        layout.append([])
        for part in parts:
            layout[-1].append((number, part.shape[0]))
            number += 1
    steps = len(layout)

    def z_at(step, place):
        return lax.rem(place[2] + (8 - hop) + step * (2 * hop - 8), 8)

    whole = lambda shape: pl.BlockSpec(shape, lambda step, place: (0,) * len(shape))
    blocks = [part for parts in mine for part in parts] + [part for parts in theirs for part in parts]
    operands = [place, weights, table, turns, *blocks]
    in_specs = [whole((8, 256, 256)), whole((128, 128))]
    in_specs += [pl.BlockSpec((1, 288, 128), lambda step, place: (z_at(step, place), 0, 0))]
    in_specs += [whole(block.shape) for block in blocks]
    aliases = {}
    if previous is not None:
        aliases = {len(operands): 0}
        operands.append(previous)
        in_specs.append(pl.BlockSpec(memory_space=pl.ANY))
    return pl.pallas_call(
        functools.partial(correlate_kernel, layout),
        grid_spec=pltpu.PrefetchScalarGridSpec(
            num_scalar_prefetch=1,
            grid=(steps,),
            in_specs=in_specs,
            out_specs=pl.BlockSpec(
                (STD, 4, 1, 32, LAGW), lambda step, place: (0, 0, z_at(step, place), 0, 0)
            ),
            scratch_shapes=[pltpu.VMEM((steps, 8, 256, 128), jnp.float32)],
        ),
        out_shape=jax.ShapeDtypeStruct((STD, 4, 8, 32, LAGW), jnp.float32),
        input_output_aliases=aliases,
        compiler_params=pltpu.CompilerParams(
            vmem_limit_bytes=24 * 1024 * 1024, dimension_semantics=("arbitrary",)
        ),
        cost_estimate=pl.CostEstimate(
            flops=cost, bytes_accessed=1 << 16, transcendentals=0
        ),
        name="correlate",
    )(*operands)


def shift(value, axis, size, by):
    return lax.ppermute(value, axis, [(at, (at + by) % size) for at in range(size)])


def per_device(raw_traces, fir_taps, source_slot, present, lag_start):
    ylo, yhi = lax.axis_index("ylo"), lax.axis_index("yhi")
    place = jnp.stack([lax.axis_index(name) for name in ("x", "core", "z", "yhi")])
    white = whiten(fir_taps.reshape(1, TAPS), raw_traces[0])
    white, lag = lax.optimization_barrier((white, lag_start))
    received = lax.all_to_all(white, STA, split_axis=0, concat_axis=0, tiled=True)
    slots = jnp.where(present != 0, source_slot, -1)
    received, place, slots, turns, table = lax.optimization_barrier(
        (received, place, slots, *phases(place, lag))
    )
    mine = select(slots, received)

    ring = lax.ppermute(mine, ("ylo", "yhi"), [(0, 2), (2, 3), (3, 1), (1, 0)])
    middle = lax.ppermute(mine, ("ylo", "yhi"), [(1, 2), (2, 1)])
    y = 2 * yhi + ylo
    early = jnp.where(y == 0, mine, jnp.where(y == 2, middle, ring))
    late = jnp.where(y == 3, mine, jnp.where(y == 1, middle, ring))
    block = jnp.stack([early, late])
    block, mine = lax.optimization_barrier((block, mine))
    other = shift(mine, "yhi", 2, 1)
    blocks = [block] + [shift(block, "x", 4, -by) for by in (1, 2, 3)]
    blocks, other = lax.optimization_barrier((blocks, other))
    line = jnp.stack(blocks)
    weights = pair_weights(yhi.reshape(1), mine, other)

    across = lambda value: shift(value, "core", 2, 1)
    up = down = line
    hops = [[[line]]]
    for _ in range(3):
        up, down = shift(up, "z", 8, 1), shift(down, "z", 8, -1)
        hops.append([[up], [down]])
    hops.append([[shift(up[:2], "z", 8, 1), shift(down[2:], "z", 8, -1)]])
    out = None
    for hop, mine_here in enumerate(hops):
        ready = mine_here
        if hop in (1, 2):
            ready, out = lax.optimization_barrier((mine_here, out))
        theirs = [[across(part) for part in parts] for parts in ready]
        out = correlate(place, weights, table, turns, out, hop, mine_here, theirs)
    return out.reshape(STD, HALF, LAGW)


def solution(mesh):
    fine = Mesh(mesh.devices.reshape(2, 4, 8, 2, 2), STA + ("yhi",))
    placed = (P("yhi", STA, None), P(), P("yhi", STA), P("yhi", STA), P(STA, None))
    return jax.shard_map(
        per_device, mesh=fine, in_specs=placed, out_specs=P(STA, "yhi", None), check_vma=False
    )
```

```python
import functools
import math

import jax
import jax.numpy as jnp
import ml_dtypes
import numpy as np
from jax import lax
from jax.experimental import pallas as pl
from jax.experimental.pallas import tpu as pltpu
from jax.sharding import Mesh, PartitionSpec as P

L = 4096
TAPS = 127
FB = 64
BIN0 = 16
LAGW = 128
STD = 16
WDEV = 8
HALF = 1024

smooth_half = 4
floor_share = 0.25
spread_eps = 1e-06

column = np.arange(128)
column_bin = column // 16 * 8 + column % 8
column_im = column // 8 % 2

STA = ("ylo", "x", "z", "core")


def unit_angle(product):
    return ((product % L).astype(np.float32) * np.float32(2.0 * math.pi / L)).astype(np.float64)


def dft_table():
    angle = unit_angle(np.arange(L)[:, None] * (BIN0 + column_bin)[None, :])
    table = np.where(column_im == 0, np.cos(angle), -np.sin(angle))
    return table.astype(np.float32).astype(ml_dtypes.bfloat16)


def lag_table():
    angle = unit_angle((BIN0 + column_bin)[:, None] * np.arange(LAGW)[None, :])
    table = np.where(column_im[:, None] == 0, np.cos(angle), -np.sin(angle))
    return (table / math.sqrt(FB * 16)).astype(np.float32).astype(ml_dtypes.bfloat16)


def band_table():
    near = np.abs(column_bin[:, None] - column_bin[None, :]) <= smooth_half
    counts = (
        np.minimum(column_bin + smooth_half, FB - 1) - np.maximum(column_bin - smooth_half, 0) + 1
    )
    band = np.where(near & (column_im[:, None] == 0), 1.0, 0.0).astype(np.float32)
    return band, (1.0 / counts).astype(np.float32)[None, :]


def swap_parts(values):
    lane = lax.broadcasted_iota(jnp.int32, values.shape, 1)
    first = (lane // 8) % 2 == 0
    width = values.shape[1]
    return jnp.where(first, pltpu.roll(values, width - 8, 1), pltpu.roll(values, 8, 1))


def whiten_kernel(taps_ref, raw_hbm, basis_hbm, band_ref, inverse_ref, out_ref, raw_ref, basis_ref, wide, sems):
    raw_copies = []
    for chunk in range(8):
        columns = slice(chunk * 512, (chunk + 1) * 512)
        raw_copies.append(
            pltpu.make_async_copy(raw_hbm.at[:, columns], raw_ref.at[:, columns], sems.at[chunk])
        )
    basis_copy = pltpu.make_async_copy(basis_hbm, basis_ref, sems.at[8])
    for chunk, raw_copy in enumerate(raw_copies):
        raw_copy.start()
        if chunk == 3:
            basis_copy.start()

    wide[...] = jnp.zeros((1, 512), jnp.float32)
    wide[:, :TAPS] = taps_ref[...].astype(jnp.float32)
    taps = jnp.broadcast_to(wide[...], (128, 512))
    chunks = []
    for chunk in range(4):
        first_shift = 128 * (chunk - 1) - 63
        moved = pltpu.roll(taps, first_shift % 512, 1, stride=1, stride_axis=0)
        chunks.append(moved[:, :256].astype(jnp.bfloat16))
    fir = jnp.concatenate(chunks, axis=0)
    fir_halves = fir[:256], fir[256:]
    edge = jnp.zeros((256, 128), jnp.bfloat16)
    spectrum = jnp.zeros((256, 128), jnp.float32)
    arrived = 0
    for group in range(4):
        tiles = range(group * 4, (group + 1) * 4)
        while arrived < 8 and arrived * 512 < tiles[-1] * 256 + 384:
            raw_copies[arrived].wait()
            arrived += 1
        filtered = jnp.zeros((256 * 4, 256), jnp.float32)
        for half in range(2):
            parts = []
            for tile in tiles:
                low = 256 * tile - 128 + 256 * half
                if low < 0:
                    parts.append(jnp.concatenate([edge, raw_ref[:, :128]], axis=1))
                elif low + 256 > L:
                    parts.append(jnp.concatenate([raw_ref[:, low:], edge], axis=1))
                else:
                    parts.append(raw_ref[:, low : low + 256])
            filtered += jnp.dot(
                jnp.concatenate(parts, axis=0),
                fir_halves[half],
                preferred_element_type=jnp.float32,
            )
        filtered = filtered.astype(jnp.bfloat16)
        if group == 0:
            basis_copy.wait()
        for number, tile in enumerate(tiles):
            spectrum += jnp.dot(
                filtered[256 * number : 256 * (number + 1)],
                basis_ref[256 * tile : 256 * (tile + 1), :],
                preferred_element_type=jnp.float32,
            )
    square = spectrum * spectrum
    magnitude = jnp.sqrt(square + swap_parts(square))
    amplitude = (
        jnp.dot(
            magnitude,
            band_ref[...],
            precision=lax.Precision.HIGHEST,
            preferred_element_type=jnp.float32,
        )
        * inverse_ref[...]
    )
    spread = jnp.sqrt(jnp.sum(square, axis=1, keepdims=True) * (1.0 / FB) + spread_eps)
    divisor = jnp.maximum(amplitude, floor_share * spread)
    out_ref[...] = (spectrum / divisor).astype(jnp.bfloat16)


def whiten(taps, raw):
    band, inverse = band_table()
    return pl.pallas_call(
        whiten_kernel,
        out_shape=jax.ShapeDtypeStruct((256, 128), jnp.bfloat16),
        in_specs=[
            pl.BlockSpec(memory_space=pltpu.VMEM),
            pl.BlockSpec(memory_space=pl.ANY),
            pl.BlockSpec(memory_space=pl.ANY),
            pl.BlockSpec(memory_space=pltpu.VMEM),
            pl.BlockSpec(memory_space=pltpu.VMEM),
        ],
        scratch_shapes=[
            pltpu.VMEM((256, L), jnp.bfloat16),
            pltpu.VMEM((L, 128), jnp.bfloat16),
            pltpu.VMEM((1, 512), jnp.float32),
            pltpu.SemaphoreType.DMA((9,)),
        ],
        compiler_params=pltpu.CompilerParams(vmem_limit_bytes=56 * 1024 * 1024),
        name="whiten",
    )(taps, raw, jnp.asarray(dft_table()), jnp.asarray(band), jnp.asarray(inverse))


def select_kernel(slot_ref, rows_ref, out_ref):
    slots = slot_ref[...]
    entry = lax.broadcasted_iota(jnp.int32, (256, STD), 0)
    stored = rows_ref[...]
    chosen = []
    for window in range(WDEV):
        picked = jnp.where(entry == slots[window : window + 1, :], 1.0, 0.0).astype(jnp.bfloat16)
        chosen.append(
            lax.dot_general(
                picked, stored, (((0,), (0,)), ((), ())), preferred_element_type=jnp.float32
            )
        )
    lane = lax.broadcasted_iota(jnp.int32, (STD, 128), 1) // 16
    for group in range(8):
        packed = jnp.zeros((STD, 128), jnp.float32)
        for window in range(WDEV):
            rows = chosen[window]
            moved = pltpu.roll(rows, (window - group) * 16 % 128, 1) if window != group else rows
            packed = jnp.where(lane == window, moved, packed)
        out_ref[:, group * 128 : (group + 1) * 128] = packed.astype(jnp.bfloat16)


def select(slots, rows):
    return pl.pallas_call(
        select_kernel,
        out_shape=jax.ShapeDtypeStruct((STD, 1024), jnp.bfloat16),
        compiler_params=pltpu.CompilerParams(vmem_limit_bytes=4 * 1024 * 1024),
        name="select",
    )(slots, rows)


cos_terms = (0.999999211, -19.7389804, 64.9286574, -85.2716215, 58.7904921, -21.0711056)
sin_terms = (6.28318492, -41.3415892, 81.5999433, -76.6144725, 41.3428824, -12.4712435)


def cos_sin(steps):
    turn = steps * (1.0 / L)
    turn = turn - jnp.round(turn)
    square = turn * turn
    cosine = jnp.full_like(square, cos_terms[-1])
    sine = jnp.full_like(square, sin_terms[-1])
    for cos_term, sin_term in zip(cos_terms[-2::-1], sin_terms[-2::-1]):
        cosine = cosine * square + cos_term
        sine = sine * square + sin_term
    return cosine, sine * turn


def phase_kernel(place_ref, lag_ref, table_ref, out_ref, table_out_ref):
    table_out_ref[...] = table_ref[...]
    x, core = place_ref[0], place_ref[1]
    lane = lax.broadcasted_iota(jnp.int32, (STD, 128), 1)
    bins = (lax.broadcasted_iota(jnp.int32, (8, 128), 0) + BIN0).astype(jnp.float32)
    for z in range(8):
        tile = jnp.zeros((STD, 128), jnp.int32)
        for x_at in range(4):
            first = (x_at * 256 + z * 32) // 128 * 128
            part = lag_ref[:, first : first + 128]
            by = (x_at - z % 4) * 32 % 128
            tile = jnp.where(lane // 32 == x_at, pltpu.roll(part, by, 1) if by else part, tile)
        tile = pltpu.roll(tile, lax.rem(128 - 32 * x, 128), 1)
        crossed = jnp.where((lane // 16) % 2 == 0, pltpu.roll(tile, 112, 1), pltpu.roll(tile, 16, 1))
        lag = jnp.where(core == 1, crossed, tile).astype(jnp.float32)
        out_ref[z, 256:272, :], out_ref[z, 272:288, :] = cos_sin(lag * 8.0)
        for station in range(STD):
            low, high = station * 8, station * 8 + 8
            steps = jnp.broadcast_to(lag[station : station + 1], (8, 128)) * bins
            out_ref[z, low:high, :], out_ref[z, 128 + low : 128 + high, :] = cos_sin(steps)


def phases(place, lag):
    return pl.pallas_call(
        phase_kernel,
        grid_spec=pltpu.PrefetchScalarGridSpec(
            num_scalar_prefetch=1,
            grid=(1,),
            in_specs=[
                pl.BlockSpec((STD, HALF), lambda step, place: (0, place[3])),
                pl.BlockSpec((128, 128), lambda step, place: (0, 0)),
            ],
            out_specs=[
                pl.BlockSpec((8, 288, 128), lambda step, place: (0, 0, 0)),
                pl.BlockSpec((128, 128), lambda step, place: (0, 0)),
            ],
        ),
        compiler_params=pltpu.CompilerParams(vmem_limit_bytes=8 * 1024 * 1024),
        out_shape=[
            jax.ShapeDtypeStruct((8, 288, 128), jnp.float32),
            jax.ShapeDtypeStruct((128, 128), jnp.bfloat16),
        ],
        cost_estimate=pl.CostEstimate(flops=1 << 20, bytes_accessed=1 << 16, transcendentals=0),
        name="phases",
    )(place, lag, jnp.asarray(lag_table()))


def weight_kernel(yhi_ref, mine_ref, other_ref, out_ref):
    mine_first = yhi_ref[0] == 0
    own_lane = lax.broadcasted_iota(jnp.int32, (8, 256), 1)
    same_bin = own_lane % 8 == lax.broadcasted_iota(jnp.int32, (8, 256), 0)
    first = (lax.broadcasted_iota(jnp.int32, (STD, 256), 1) // 8) % 2 == 0
    for group in range(8):
        lanes = slice(group * 128, (group + 1) * 128)
        mine = mine_ref[:, lanes].astype(jnp.float32)
        other = other_ref[:, lanes].astype(jnp.float32)
        early = jnp.where(mine_first, mine, other)
        own = jnp.concatenate([early, jnp.where(mine_first, other, mine)], axis=1)
        swapped = swap_parts(own)
        swapped = jnp.where(first, swapped, -swapped)
        rows = []
        for station in range(STD):
            for part in (own, swapped):
                row = jnp.broadcast_to(part[station : station + 1], (8, 256))
                rows.append(jnp.where(same_bin, row, 0.0))
        out_ref[group] = jnp.concatenate(rows, axis=0).astype(jnp.bfloat16)


def pair_weights(yhi, mine, other):
    return pl.pallas_call(
        weight_kernel,
        in_specs=[
            pl.BlockSpec(memory_space=pltpu.SMEM),
            pl.BlockSpec(memory_space=pltpu.VMEM),
            pl.BlockSpec(memory_space=pltpu.VMEM),
        ],
        out_shape=jax.ShapeDtypeStruct((8, 256, 256), jnp.bfloat16),
        compiler_params=pltpu.CompilerParams(vmem_limit_bytes=8 * 1024 * 1024),
        cost_estimate=pl.CostEstimate(flops=1 << 20, bytes_accessed=1 << 16, transcendentals=0),
        name="pair_weights",
    )(yhi, mine, other)


def correlate_kernel(layout, place_ref, weight_ref, table_ref, turn_ref, *rest):
    count = sum(len(parts) for parts in layout)
    mine, theirs = rest[:count], rest[count : 2 * count]
    out_ref, cross = rest[-2:]
    step = pl.program_id(0)
    x, core = place_ref[0], place_ref[1]

    @pl.when(step == 0)
    def _():
        for group in range(8):
            lanes = slice(group * 128, (group + 1) * 128)
            halves = []
            for half in range(2):
                blocks = []
                for parts in layout:
                    for number, rows in parts:
                        for row in range(rows):
                            blocks.append(mine[number][row, half, :, lanes])
                            blocks.append(theirs[number][row, half, :, lanes])
                halves.append(jnp.concatenate(blocks, axis=0))
            product = lax.dot_general(
                weight_ref[group],
                jnp.concatenate(halves, axis=1),
                (((1,), (1,)), ((), ())),
                preferred_element_type=jnp.float32,
            )
            for at in range(len(layout)):
                cross[at, group] = product[:, at * 128 : (at + 1) * 128]

    for station in range(STD):
        top = station * 16
        cosine = turn_ref[0, station * 8 : station * 8 + 8, :]
        sine = turn_ref[0, station * 8 + 128 : station * 8 + 136, :]
        cos_next = jnp.broadcast_to(turn_ref[0, station + 256 : station + 257, :], (8, 128))
        sin_next = jnp.broadcast_to(turn_ref[0, station + 272 : station + 273, :], (8, 128))
        rotated = []
        for group in range(8):
            real = cross[step, group, top : top + 8, :]
            imag = cross[step, group, top + 8 : top + 16, :]
            rotated.append(real * cosine - imag * sine)
            rotated.append(real * sine + imag * cosine)
            if group < 7:
                cosine, sine = (
                    cosine * cos_next - sine * sin_next,
                    cosine * sin_next + sine * cos_next,
                )
        rotated = jnp.concatenate(rotated, axis=0).astype(jnp.bfloat16)
        values = lax.dot_general(
            rotated, table_ref[...], (((0,), (0,)), ((), ())), preferred_element_type=jnp.float32
        )
        for ahead in range(4):
            for other in range(2):
                row = pl.multiple_of(lax.rem(core + other, 2) * 16, 16)
                first = ahead * 32 + other * 16
                out_ref[station, lax.rem(x + ahead, 4), 0, pl.ds(row, 16), :] = values[
                    first : first + 16
                ]


def correlate(place, weights, table, turns, previous, hop, mine, theirs):
    cost = (1 << 31, 1 << 30, 1 << 28, 1 << 31, 1 << 30)[hop]
    layout, number = [], 0
    for parts in mine:
        layout.append([])
        for part in parts:
            layout[-1].append((number, part.shape[0]))
            number += 1
    steps = len(layout)

    def z_at(step, place):
        return lax.rem(place[2] + (8 - hop) + step * (2 * hop - 8), 8)

    whole = lambda shape: pl.BlockSpec(shape, lambda step, place: (0,) * len(shape))
    blocks = [part for parts in mine for part in parts] + [part for parts in theirs for part in parts]
    operands = [place, weights, table, turns, *blocks]
    in_specs = [whole((8, 256, 256)), whole((128, 128))]
    in_specs += [pl.BlockSpec((1, 288, 128), lambda step, place: (z_at(step, place), 0, 0))]
    in_specs += [whole(block.shape) for block in blocks]
    aliases = {}
    if previous is not None:
        aliases = {len(operands): 0}
        operands.append(previous)
        in_specs.append(pl.BlockSpec(memory_space=pl.ANY))
    return pl.pallas_call(
        functools.partial(correlate_kernel, layout),
        grid_spec=pltpu.PrefetchScalarGridSpec(
            num_scalar_prefetch=1,
            grid=(steps,),
            in_specs=in_specs,
            out_specs=pl.BlockSpec(
                (STD, 4, 1, 32, LAGW), lambda step, place: (0, 0, z_at(step, place), 0, 0)
            ),
            scratch_shapes=[pltpu.VMEM((steps, 8, 256, 128), jnp.float32)],
        ),
        out_shape=jax.ShapeDtypeStruct((STD, 4, 8, 32, LAGW), jnp.float32),
        input_output_aliases=aliases,
        compiler_params=pltpu.CompilerParams(
            vmem_limit_bytes=24 * 1024 * 1024, dimension_semantics=("arbitrary",)
        ),
        cost_estimate=pl.CostEstimate(
            flops=cost, bytes_accessed=1 << 16, transcendentals=0
        ),
        name="correlate",
    )(*operands)


def shift(value, axis, size, by):
    return lax.ppermute(value, axis, [(at, (at + by) % size) for at in range(size)])


def per_device(raw_traces, fir_taps, source_slot, present, lag_start):
    ylo, yhi = lax.axis_index("ylo"), lax.axis_index("yhi")
    place = jnp.stack([lax.axis_index(name) for name in ("x", "core", "z", "yhi")])
    white = whiten(fir_taps.reshape(1, TAPS), raw_traces[0])
    received = lax.all_to_all(white, STA, split_axis=0, concat_axis=0, tiled=True)
    slots = jnp.where(present != 0, source_slot, -1)
    received, slots = lax.optimization_barrier((received, slots))
    mine = select(slots, received)

    ring = lax.ppermute(mine, ("ylo", "yhi"), [(0, 2), (2, 3), (3, 1), (1, 0)])
    middle = lax.ppermute(mine, ("ylo", "yhi"), [(1, 2), (2, 1)])
    y = 2 * yhi + ylo
    early = jnp.where(y == 0, mine, jnp.where(y == 2, middle, ring))
    late = jnp.where(y == 3, mine, jnp.where(y == 1, middle, ring))
    block = jnp.stack([early, late])
    block, mine = lax.optimization_barrier((block, mine))
    other = shift(mine, "yhi", 2, 1)
    blocks = [block] + [shift(block, "x", 4, -by) for by in (1, 2, 3)]
    blocks, other = lax.optimization_barrier((blocks, other))
    line, place, lag_start = lax.optimization_barrier((jnp.stack(blocks), place, lag_start))
    turns, table = phases(place, lag_start)
    weights = pair_weights(yhi.reshape(1), mine, other)

    across = lambda value: shift(value, "core", 2, 1)
    up = down = line
    hops = [[[line]]]
    for _ in range(3):
        up, down = shift(up, "z", 8, 1), shift(down, "z", 8, -1)
        hops.append([[up], [down]])
    hops.append([[shift(up[:2], "z", 8, 1), shift(down[2:], "z", 8, -1)]])
    out = None
    for hop, mine_here in enumerate(hops):
        ready = mine_here
        if hop in (1, 2):
            ready, out = lax.optimization_barrier((mine_here, out))
        theirs = [[across(part) for part in parts] for parts in ready]
        out = correlate(place, weights, table, turns, out, hop, mine_here, theirs)
    return out.reshape(STD, HALF, LAGW)


def solution(mesh):
    fine = Mesh(mesh.devices.reshape(2, 4, 8, 2, 2), STA + ("yhi",))
    placed = (P("yhi", STA, None), P(), P("yhi", STA), P("yhi", STA), P(STA, None))
    return jax.shard_map(
        per_device, mesh=fine, in_specs=placed, out_specs=P(STA, "yhi", None), check_vma=False
    )
```

```python
import functools
import math

import jax
import jax.numpy as jnp
import ml_dtypes
import numpy as np
from jax import lax
from jax.experimental import pallas as pl
from jax.experimental.pallas import tpu as pltpu
from jax.sharding import Mesh, PartitionSpec as P

L = 4096
TAPS = 127
FB = 64
BIN0 = 16
LAGW = 128
STD = 16
WDEV = 8
HALF = 1024

smooth_half = 4
floor_share = 0.25
spread_eps = 1e-06

column = np.arange(128)
column_bin = column // 16 * 8 + column % 8
column_im = column // 8 % 2

STA = ("ylo", "x", "z", "core")


def unit_angle(product):
    return ((product % L).astype(np.float32) * np.float32(2.0 * math.pi / L)).astype(np.float64)


def dft_table():
    angle = unit_angle(np.arange(L)[:, None] * (BIN0 + column_bin)[None, :])
    table = np.where(column_im == 0, np.cos(angle), -np.sin(angle))
    return table.astype(np.float32).astype(ml_dtypes.bfloat16)


def lag_table():
    angle = unit_angle((BIN0 + column_bin)[:, None] * np.arange(LAGW)[None, :])
    table = np.where(column_im[:, None] == 0, np.cos(angle), -np.sin(angle))
    return (table / math.sqrt(FB * 16)).astype(np.float32).astype(ml_dtypes.bfloat16)


def band_table():
    near = np.abs(column_bin[:, None] - column_bin[None, :]) <= smooth_half
    counts = (
        np.minimum(column_bin + smooth_half, FB - 1) - np.maximum(column_bin - smooth_half, 0) + 1
    )
    band = np.where(near & (column_im[:, None] == 0), 1.0, 0.0).astype(np.float32)
    return band, (1.0 / counts).astype(np.float32)[None, :]


def swap_parts(values):
    lane = lax.broadcasted_iota(jnp.int32, values.shape, 1)
    first = (lane // 8) % 2 == 0
    width = values.shape[1]
    return jnp.where(first, pltpu.roll(values, width - 8, 1), pltpu.roll(values, 8, 1))


def whiten_kernel(taps_ref, raw_hbm, basis_hbm, band_ref, inverse_ref, out_ref, raw_ref, basis_ref, wide, sems):
    raw_copies = []
    for chunk in range(8):
        columns = slice(chunk * 512, (chunk + 1) * 512)
        raw_copies.append(
            pltpu.make_async_copy(raw_hbm.at[:, columns], raw_ref.at[:, columns], sems.at[chunk])
        )
    basis_copy = pltpu.make_async_copy(basis_hbm, basis_ref, sems.at[8])
    for chunk, raw_copy in enumerate(raw_copies):
        raw_copy.start()
        if chunk == 3:
            basis_copy.start()

    wide[...] = jnp.zeros((1, 512), jnp.float32)
    wide[:, :TAPS] = taps_ref[...].astype(jnp.float32)
    taps = jnp.broadcast_to(wide[...], (128, 512))
    chunks = []
    for chunk in range(4):
        first_shift = 128 * (chunk - 1) - 63
        moved = pltpu.roll(taps, first_shift % 512, 1, stride=1, stride_axis=0)
        chunks.append(moved[:, :256].astype(jnp.bfloat16))
    fir = jnp.concatenate(chunks, axis=0)
    fir_halves = fir[:256], fir[256:]
    edge = jnp.zeros((256, 128), jnp.bfloat16)
    spectrum = jnp.zeros((256, 128), jnp.float32)
    arrived = 0
    for group in range(4):
        tiles = range(group * 4, (group + 1) * 4)
        while arrived < 8 and arrived * 512 < tiles[-1] * 256 + 384:
            raw_copies[arrived].wait()
            arrived += 1
        filtered = jnp.zeros((256 * 4, 256), jnp.float32)
        for half in range(2):
            parts = []
            for tile in tiles:
                low = 256 * tile - 128 + 256 * half
                if low < 0:
                    parts.append(jnp.concatenate([edge, raw_ref[:, :128]], axis=1))
                elif low + 256 > L:
                    parts.append(jnp.concatenate([raw_ref[:, low:], edge], axis=1))
                else:
                    parts.append(raw_ref[:, low : low + 256])
            filtered += jnp.dot(
                jnp.concatenate(parts, axis=0),
                fir_halves[half],
                preferred_element_type=jnp.float32,
            )
        filtered = filtered.astype(jnp.bfloat16)
        if group == 0:
            basis_copy.wait()
        samples = [filtered[256 * number : 256 * (number + 1)] for number in range(4)]
        spectrum += jnp.dot(
            jnp.concatenate(samples, axis=1),
            basis_ref[1024 * group : 1024 * (group + 1), :],
            preferred_element_type=jnp.float32,
        )
    square = spectrum * spectrum
    magnitude = jnp.sqrt(square + swap_parts(square))
    amplitude = (
        jnp.dot(
            magnitude,
            band_ref[...],
            precision=lax.Precision.HIGHEST,
            preferred_element_type=jnp.float32,
        )
        * inverse_ref[...]
    )
    spread = jnp.sqrt(jnp.sum(square, axis=1, keepdims=True) * (1.0 / FB) + spread_eps)
    divisor = jnp.maximum(amplitude, floor_share * spread)
    out_ref[...] = (spectrum / divisor).astype(jnp.bfloat16)


def whiten(taps, raw):
    band, inverse = band_table()
    return pl.pallas_call(
        whiten_kernel,
        out_shape=jax.ShapeDtypeStruct((256, 128), jnp.bfloat16),
        in_specs=[
            pl.BlockSpec(memory_space=pltpu.VMEM),
            pl.BlockSpec(memory_space=pl.ANY),
            pl.BlockSpec(memory_space=pl.ANY),
            pl.BlockSpec(memory_space=pltpu.VMEM),
            pl.BlockSpec(memory_space=pltpu.VMEM),
        ],
        scratch_shapes=[
            pltpu.VMEM((256, L), jnp.bfloat16),
            pltpu.VMEM((L, 128), jnp.bfloat16),
            pltpu.VMEM((1, 512), jnp.float32),
            pltpu.SemaphoreType.DMA((9,)),
        ],
        compiler_params=pltpu.CompilerParams(vmem_limit_bytes=56 * 1024 * 1024),
        name="whiten",
    )(taps, raw, jnp.asarray(dft_table()), jnp.asarray(band), jnp.asarray(inverse))


def select_kernel(slot_ref, rows_ref, out_ref):
    slots = slot_ref[...]
    entry = lax.broadcasted_iota(jnp.int32, (256, STD), 0)
    stored = rows_ref[...]
    chosen = []
    for window in range(WDEV):
        picked = jnp.where(entry == slots[window : window + 1, :], 1.0, 0.0).astype(jnp.bfloat16)
        chosen.append(
            lax.dot_general(
                picked, stored, (((0,), (0,)), ((), ())), preferred_element_type=jnp.float32
            )
        )
    lane = lax.broadcasted_iota(jnp.int32, (STD, 128), 1) // 16
    for group in range(8):
        packed = jnp.zeros((STD, 128), jnp.float32)
        for window in range(WDEV):
            rows = chosen[window]
            moved = pltpu.roll(rows, (window - group) * 16 % 128, 1) if window != group else rows
            packed = jnp.where(lane == window, moved, packed)
        out_ref[:, group * 128 : (group + 1) * 128] = packed.astype(jnp.bfloat16)


def select(slots, rows):
    return pl.pallas_call(
        select_kernel,
        out_shape=jax.ShapeDtypeStruct((STD, 1024), jnp.bfloat16),
        compiler_params=pltpu.CompilerParams(vmem_limit_bytes=4 * 1024 * 1024),
        name="select",
    )(slots, rows)


cos_terms = (0.999999211, -19.7389804, 64.9286574, -85.2716215, 58.7904921, -21.0711056)
sin_terms = (6.28318492, -41.3415892, 81.5999433, -76.6144725, 41.3428824, -12.4712435)


def cos_sin(steps):
    turn = steps * (1.0 / L)
    turn = turn - jnp.round(turn)
    square = turn * turn
    cosine = jnp.full_like(square, cos_terms[-1])
    sine = jnp.full_like(square, sin_terms[-1])
    for cos_term, sin_term in zip(cos_terms[-2::-1], sin_terms[-2::-1]):
        cosine = cosine * square + cos_term
        sine = sine * square + sin_term
    return cosine, sine * turn


def phase_kernel(place_ref, lag_ref, table_ref, out_ref, table_out_ref):
    table_out_ref[...] = table_ref[...]
    x, core = place_ref[0], place_ref[1]
    lane = lax.broadcasted_iota(jnp.int32, (STD, 128), 1)
    bins = (lax.broadcasted_iota(jnp.int32, (8, 128), 0) + BIN0).astype(jnp.float32)
    for z in range(8):
        tile = jnp.zeros((STD, 128), jnp.int32)
        for x_at in range(4):
            first = (x_at * 256 + z * 32) // 128 * 128
            part = lag_ref[:, first : first + 128]
            by = (x_at - z % 4) * 32 % 128
            tile = jnp.where(lane // 32 == x_at, pltpu.roll(part, by, 1) if by else part, tile)
        tile = pltpu.roll(tile, lax.rem(128 - 32 * x, 128), 1)
        crossed = jnp.where((lane // 16) % 2 == 0, pltpu.roll(tile, 112, 1), pltpu.roll(tile, 16, 1))
        lag = jnp.where(core == 1, crossed, tile).astype(jnp.float32)
        out_ref[z, 256:272, :], out_ref[z, 272:288, :] = cos_sin(lag * 8.0)
        for station in range(STD):
            low, high = station * 8, station * 8 + 8
            steps = jnp.broadcast_to(lag[station : station + 1], (8, 128)) * bins
            out_ref[z, low:high, :], out_ref[z, 128 + low : 128 + high, :] = cos_sin(steps)


def phases(place, lag):
    return pl.pallas_call(
        phase_kernel,
        grid_spec=pltpu.PrefetchScalarGridSpec(
            num_scalar_prefetch=1,
            grid=(1,),
            in_specs=[
                pl.BlockSpec((STD, HALF), lambda step, place: (0, place[3])),
                pl.BlockSpec((128, 128), lambda step, place: (0, 0)),
            ],
            out_specs=[
                pl.BlockSpec((8, 288, 128), lambda step, place: (0, 0, 0)),
                pl.BlockSpec((128, 128), lambda step, place: (0, 0)),
            ],
        ),
        compiler_params=pltpu.CompilerParams(vmem_limit_bytes=8 * 1024 * 1024),
        out_shape=[
            jax.ShapeDtypeStruct((8, 288, 128), jnp.float32),
            jax.ShapeDtypeStruct((128, 128), jnp.bfloat16),
        ],
        cost_estimate=pl.CostEstimate(flops=1 << 20, bytes_accessed=1 << 16, transcendentals=0),
        name="phases",
    )(place, lag, jnp.asarray(lag_table()))


def weight_kernel(yhi_ref, mine_ref, other_ref, out_ref):
    mine_first = yhi_ref[0] == 0
    own_lane = lax.broadcasted_iota(jnp.int32, (8, 256), 1)
    same_bin = own_lane % 8 == lax.broadcasted_iota(jnp.int32, (8, 256), 0)
    first = (lax.broadcasted_iota(jnp.int32, (STD, 256), 1) // 8) % 2 == 0
    for group in range(8):
        lanes = slice(group * 128, (group + 1) * 128)
        mine = mine_ref[:, lanes].astype(jnp.float32)
        other = other_ref[:, lanes].astype(jnp.float32)
        early = jnp.where(mine_first, mine, other)
        own = jnp.concatenate([early, jnp.where(mine_first, other, mine)], axis=1)
        swapped = swap_parts(own)
        swapped = jnp.where(first, swapped, -swapped)
        rows = []
        for station in range(STD):
            for part in (own, swapped):
                row = jnp.broadcast_to(part[station : station + 1], (8, 256))
                rows.append(jnp.where(same_bin, row, 0.0))
        out_ref[group] = jnp.concatenate(rows, axis=0).astype(jnp.bfloat16)


def pair_weights(yhi, mine, other):
    return pl.pallas_call(
        weight_kernel,
        in_specs=[
            pl.BlockSpec(memory_space=pltpu.SMEM),
            pl.BlockSpec(memory_space=pltpu.VMEM),
            pl.BlockSpec(memory_space=pltpu.VMEM),
        ],
        out_shape=jax.ShapeDtypeStruct((8, 256, 256), jnp.bfloat16),
        compiler_params=pltpu.CompilerParams(vmem_limit_bytes=8 * 1024 * 1024),
        cost_estimate=pl.CostEstimate(flops=1 << 20, bytes_accessed=1 << 16, transcendentals=0),
        name="pair_weights",
    )(yhi, mine, other)


def correlate_kernel(layout, place_ref, weight_ref, table_ref, turn_ref, *rest):
    count = sum(len(parts) for parts in layout)
    mine, theirs = rest[:count], rest[count : 2 * count]
    out_ref, cross = rest[-2:]
    step = pl.program_id(0)
    x, core = place_ref[0], place_ref[1]

    @pl.when(step == 0)
    def _():
        for group in range(8):
            lanes = slice(group * 128, (group + 1) * 128)
            halves = []
            for half in range(2):
                blocks = []
                for parts in layout:
                    for number, rows in parts:
                        for row in range(rows):
                            blocks.append(mine[number][row, half, :, lanes])
                            blocks.append(theirs[number][row, half, :, lanes])
                halves.append(jnp.concatenate(blocks, axis=0))
            product = lax.dot_general(
                weight_ref[group],
                jnp.concatenate(halves, axis=1),
                (((1,), (1,)), ((), ())),
                preferred_element_type=jnp.float32,
            )
            for at in range(len(layout)):
                cross[at, group] = product[:, at * 128 : (at + 1) * 128]

    for station in range(STD):
        top = station * 16
        cosine = turn_ref[0, station * 8 : station * 8 + 8, :]
        sine = turn_ref[0, station * 8 + 128 : station * 8 + 136, :]
        cos_next = jnp.broadcast_to(turn_ref[0, station + 256 : station + 257, :], (8, 128))
        sin_next = jnp.broadcast_to(turn_ref[0, station + 272 : station + 273, :], (8, 128))
        rotated = []
        for group in range(8):
            real = cross[step, group, top : top + 8, :]
            imag = cross[step, group, top + 8 : top + 16, :]
            rotated.append(real * cosine - imag * sine)
            rotated.append(real * sine + imag * cosine)
            if group < 7:
                cosine, sine = (
                    cosine * cos_next - sine * sin_next,
                    cosine * sin_next + sine * cos_next,
                )
        rotated = jnp.concatenate(rotated, axis=0).astype(jnp.bfloat16)
        values = lax.dot_general(
            rotated, table_ref[...], (((0,), (0,)), ((), ())), preferred_element_type=jnp.float32
        )
        for ahead in range(4):
            for other in range(2):
                row = pl.multiple_of(lax.rem(core + other, 2) * 16, 16)
                first = ahead * 32 + other * 16
                out_ref[station, lax.rem(x + ahead, 4), 0, pl.ds(row, 16), :] = values[
                    first : first + 16
                ]


def correlate(place, weights, table, turns, previous, hop, mine, theirs):
    cost = (1 << 31, 1 << 30, 1 << 28, 1 << 31, 1 << 30)[hop]
    layout, number = [], 0
    for parts in mine:
        layout.append([])
        for part in parts:
            layout[-1].append((number, part.shape[0]))
            number += 1
    steps = len(layout)

    def z_at(step, place):
        return lax.rem(place[2] + (8 - hop) + step * (2 * hop - 8), 8)

    whole = lambda shape: pl.BlockSpec(shape, lambda step, place: (0,) * len(shape))
    blocks = [part for parts in mine for part in parts] + [part for parts in theirs for part in parts]
    operands = [place, weights, table, turns, *blocks]
    in_specs = [whole((8, 256, 256)), whole((128, 128))]
    in_specs += [pl.BlockSpec((1, 288, 128), lambda step, place: (z_at(step, place), 0, 0))]
    in_specs += [whole(block.shape) for block in blocks]
    aliases = {}
    if previous is not None:
        aliases = {len(operands): 0}
        operands.append(previous)
        in_specs.append(pl.BlockSpec(memory_space=pl.ANY))
    return pl.pallas_call(
        functools.partial(correlate_kernel, layout),
        grid_spec=pltpu.PrefetchScalarGridSpec(
            num_scalar_prefetch=1,
            grid=(steps,),
            in_specs=in_specs,
            out_specs=pl.BlockSpec(
                (STD, 4, 1, 32, LAGW), lambda step, place: (0, 0, z_at(step, place), 0, 0)
            ),
            scratch_shapes=[pltpu.VMEM((steps, 8, 256, 128), jnp.float32)],
        ),
        out_shape=jax.ShapeDtypeStruct((STD, 4, 8, 32, LAGW), jnp.float32),
        input_output_aliases=aliases,
        compiler_params=pltpu.CompilerParams(
            vmem_limit_bytes=24 * 1024 * 1024, dimension_semantics=("arbitrary",)
        ),
        cost_estimate=pl.CostEstimate(
            flops=cost, bytes_accessed=1 << 16, transcendentals=0
        ),
        name="correlate",
    )(*operands)


def shift(value, axis, size, by):
    return lax.ppermute(value, axis, [(at, (at + by) % size) for at in range(size)])


def per_device(raw_traces, fir_taps, source_slot, present, lag_start):
    ylo, yhi = lax.axis_index("ylo"), lax.axis_index("yhi")
    place = jnp.stack([lax.axis_index(name) for name in ("x", "core", "z", "yhi")])
    white = whiten(fir_taps.reshape(1, TAPS), raw_traces[0])
    white, lag = lax.optimization_barrier((white, lag_start))
    received = lax.all_to_all(white, STA, split_axis=0, concat_axis=0, tiled=True)
    slots = jnp.where(present != 0, source_slot, -1)
    received, place, slots, turns, table = lax.optimization_barrier(
        (received, place, slots, *phases(place, lag))
    )
    mine = select(slots, received)

    ring = lax.ppermute(mine, ("ylo", "yhi"), [(0, 2), (2, 3), (3, 1), (1, 0)])
    middle = lax.ppermute(mine, ("ylo", "yhi"), [(1, 2), (2, 1)])
    y = 2 * yhi + ylo
    early = jnp.where(y == 0, mine, jnp.where(y == 2, middle, ring))
    late = jnp.where(y == 3, mine, jnp.where(y == 1, middle, ring))
    block = jnp.stack([early, late])
    block, mine = lax.optimization_barrier((block, mine))
    other = shift(mine, "yhi", 2, 1)
    blocks = [block] + [shift(block, "x", 4, -by) for by in (1, 2, 3)]
    blocks, other = lax.optimization_barrier((blocks, other))
    line = jnp.stack(blocks)
    weights = pair_weights(yhi.reshape(1), mine, other)

    across = lambda value: shift(value, "core", 2, 1)
    up = down = line
    hops = [[[line]]]
    for _ in range(3):
        up, down = shift(up, "z", 8, 1), shift(down, "z", 8, -1)
        hops.append([[up], [down]])
    hops.append([[shift(up[:2], "z", 8, 1), shift(down[2:], "z", 8, -1)]])
    out = None
    for hop, mine_here in enumerate(hops):
        ready = mine_here
        if hop in (1, 2):
            ready, out = lax.optimization_barrier((mine_here, out))
        theirs = [[across(part) for part in parts] for parts in ready]
        out = correlate(place, weights, table, turns, out, hop, mine_here, theirs)
    return out.reshape(STD, HALF, LAGW)


def solution(mesh):
    fine = Mesh(mesh.devices.reshape(2, 4, 8, 2, 2), STA + ("yhi",))
    placed = (P("yhi", STA, None), P(), P("yhi", STA), P("yhi", STA), P(STA, None))
    return jax.shard_map(
        per_device, mesh=fine, in_specs=placed, out_specs=P(STA, "yhi", None), check_vma=False
    )
```
